32 devices in a mesh: section: 2 (over x), dp: 4 (over z), tensor: 4 (over y, core).
Axes of the slice: x: 2, y: 2, z: 4, core: 2. Of those that a mesh axis runs over, the one named last changes fastest.
Arguments:
- inputs: bfloat16 [2, 4, 256, 1024], P(None, 'dp', 'tensor'), may hold values from -6 to 6
- cotangent: bfloat16 [2, 4, 256, 1024], P(None, 'dp', 'tensor'), may hold values from -6 to 6
- segment_ids: int32 [2, 4, 256], P(None, 'dp'), may hold values from 0 to 2, as said below
- norm_gains: bfloat16 [2, 2, 1024], P('section'), may hold values from 0.5 to 1.5
- mixer_in: bfloat16 [2, 2, 1024, 1536], P('section', None, None, 'tensor'), may hold values from -0.1875 to 0.1875
- state_proj: bfloat16 [2, 2, 1024, 128], P('section'), may hold values from -0.1875 to 0.1875
- step_proj: bfloat16 [2, 1024, 24], P('section', None, 'tensor'), may hold values from -0.1875 to 0.1875
- conv_inner: bfloat16 [2, 4, 1536], P('section', None, 'tensor'), may hold values from -3 to 3
- conv_state: bfloat16 [2, 2, 4, 128], P('section'), may hold values from -3 to 3
- head_params: float32 [2, 3, 24], P('section', None, 'tensor'), may hold values from -7 to 3
- mixer_out: bfloat16 [2, 1536, 1024], P('section', 'tensor'), may hold values from -0.15625 to 0.15625
- query_proj: bfloat16 [2, 1024, 512], P('section', None, 'tensor'), may hold values from -0.1875 to 0.1875
- keyval_proj: bfloat16 [2, 1024, 256], P('section'), may hold values from -0.1875 to 0.1875
- output_proj: bfloat16 [2, 512, 1024], P('section', 'tensor'), may hold values from -0.75 to 0.75
- gate_up: bfloat16 [2, 2, 1024, 2048], P('section', None, None, 'tensor'), may hold values from -0.1875 to 0.1875
- down_proj: bfloat16 [2, 2048, 1024], P('section', 'tensor'), may hold values from -0.125 to 0.125
Outputs:
- section_outs: bfloat16 [2, 2, 4, 256, 1024], P('section', None, 'dp', 'tensor')
- section_grads: bfloat16 [2, 2, 4, 256, 1024], P('section', None, 'dp', 'tensor')
- grad_norm_gains: float32 [2, 2, 1024], P('section', None, ('dp', 'tensor'))
- grad_mixer_in: float32 [2, 2, 1024, 1536], P('section', None, 'dp', 'tensor')
- grad_state_proj: float32 [2, 2, 1024, 128], P('section', None, ('dp', 'tensor'))
- grad_step_proj: float32 [2, 1024, 24], P('section', 'dp', 'tensor')
- grad_conv_inner: float32 [2, 4, 1536], P('section', None, 'tensor')
- grad_conv_state: float32 [2, 2, 4, 128], P('section', None, None, ('dp', 'tensor'))
- grad_head_params: float32 [2, 3, 24], P('section', None, 'tensor')
- grad_mixer_out: float32 [2, 1536, 1024], P('section', 'tensor', 'dp')
- grad_query_proj: float32 [2, 1024, 512], P('section', 'dp', 'tensor')
- grad_keyval_proj: float32 [2, 1024, 256], P('section', ('dp', 'tensor'))
- grad_output_proj: float32 [2, 512, 1024], P('section', 'tensor', 'dp')
- grad_gate_up: float32 [2, 2, 1024, 2048], P('section', None, 'dp', 'tensor')
- grad_down_proj: float32 [2, 2048, 1024], P('section', 'tensor', 'dp')
The draws below stay inside these ranges and needn't reach their ends.
Inputs may be any that keep to these rules, and one draw needn't show every extreme that they name: `segment_ids`: along each sequence the ids start at 0, never fall, and rise by at most one from one token to the next.
All inputs are finite; a program needn't handle non-finite values.
Results may differ from the reference program's by a relative error of at most 0.028.
Values may be sent and summed in bfloat16 or wider, within the bound.
No kernel may reach another device: no remote copies, remote signals or barrier semaphores. Data moves between devices by JAX's collectives and lax.ppermute only.
A program may use at most 192 MiB of HBM per device.

```python
import jax
import jax.numpy as jnp
from jax import lax

D = 1024
MH = 24
HD = 64
NS = 128
KERNEL = 4
AH = 8
KVH = 2
AD = 64
FF = 2048
SEQ = 256
MICRO = 2
BATCH = 4
N_SECTION = 2
N_TENSOR = 4


def draw_segment_ids(key, part):
    key = jax.random.fold_in(key, 11)
    first_key, second_key = jax.random.split(key)
    sequences = MICRO * BATCH
    front_len = jax.random.randint(first_key, (sequences, 1), 1, SEQ // 4)
    back_len = jax.random.randint(second_key, (sequences, 1), 1, SEQ // 4)
    places = jnp.arange(SEQ)[None, :]
    labels = (places >= front_len).astype(jnp.int32) + (places >= SEQ - back_len).astype(jnp.int32)
    return labels.reshape(MICRO, BATCH, SEQ)


def draw_head_params(key, part):
    key = jax.random.fold_in(key, 23)
    step_key, decay_key, skip_key = jax.random.split(key, 3)
    step_size = jnp.exp(jax.random.uniform(step_key, (N_SECTION, MH), jnp.float32, jnp.log(0.004), jnp.log(0.1)))
    step_bias = jnp.log(jnp.expm1(step_size))
    decay_log = jnp.log(jax.random.uniform(decay_key, (N_SECTION, MH), jnp.float32, 1.0, 16.0))
    skip_gain = jax.random.uniform(skip_key, (N_SECTION, MH), jnp.float32, 0.5, 1.5)
    return jnp.stack([step_bias, decay_log, skip_gain], axis=1).astype(jnp.float32)


def strengthened(result, stream_key, source, target, shards_of, factor):
    owner, partner = [(jnp.arange(result.shape[axis_at]) // (result.shape[axis_at] // shards_of)).reshape([-1 if axis == axis_at else 1 for axis in range(result.ndim)]) for axis_at in (source, target)]
    chosen = jax.random.permutation(stream_key, shards_of)[partner]
    strong = (owner == chosen) | (owner == (partner + shards_of // 2) % shards_of)
    return jnp.where(strong, factor * result, result)


def level_of(rng, dims, shards, least, high):
    level = 1.0
    for axis_at, parts in shards:
        draws = jax.random.uniform(jax.random.fold_in(jax.random.fold_in(rng, 6), axis_at), (parts,), jnp.float32, least / len(shards), high / len(shards))
        level = level * jnp.repeat(jnp.exp(draws), dims[axis_at] // parts).reshape((-1,) + (1,) * (len(dims) - 1 - axis_at))
    return level


def noise(rng, shape, scale, limit, shards=(), held_as=jnp.bfloat16):
    level = level_of(rng, shape, shards, -0.22, 0.18) if shards else 1.0
    drawn = jax.random.normal(rng, shape, jnp.float32) * scale * level
    return jnp.minimum(jnp.maximum(drawn, -limit), limit).astype(held_as)


def bell_draw_with(stream_key, extent, deviation, reach, cuts, heavy, held_as=jnp.bfloat16):
    drawn = deviation * jax.random.normal(stream_key, extent, jnp.float32)
    if cuts:
        drawn = drawn * level_of(stream_key, extent, cuts, -0.22, 0.18)
    return jnp.clip(strengthened(drawn, jax.random.fold_in(stream_key, 3), *heavy), -reach, reach).astype(held_as)


def setup_inputs(seed: int = 0) -> dict:
    keys = jax.random.split(jax.random.key(seed), 17)
    inputs = bell_draw_with(keys[0], (MICRO, BATCH, SEQ, D), 1.0, 6.0, ((1, 4), (2, 4)), (1, 3, 4, 2.0))
    cotangent = bell_draw_with(keys[1], (MICRO, BATCH, SEQ, D), 1.0, 6.0, ((1, 4), (2, 4)), (1, 3, 4, 2.0))
    segment_ids = draw_segment_ids(jax.random.fold_in(keys[16], 71), 0)
    norm_gains = jnp.clip(1.0 + 0.1 * jax.random.normal(keys[3], (N_SECTION, 2, D), jnp.float32), 0.5, 1.5).astype(jnp.bfloat16)
    mixer_in = noise(keys[4], (N_SECTION, 2, D, MH * HD), D ** -0.5, 0.1875, ((0, 2), (3, 4)))
    state_proj = noise(keys[5], (N_SECTION, 2, D, NS), D ** -0.5, 0.1875, ((0, 2),))
    step_proj = noise(keys[6], (N_SECTION, D, MH), D ** -0.5, 0.1875, ((0, 2), (2, 4)))
    conv_inner = noise(keys[7], (N_SECTION, KERNEL, MH * HD), KERNEL ** -0.5, 3.0, ((0, 2), (2, 4)))
    conv_state = noise(keys[8], (N_SECTION, 2, KERNEL, NS), KERNEL ** -0.5, 3.0, ((0, 2),))
    head_params = draw_head_params(jax.random.fold_in(keys[16], 71), 0)
    mixer_out = noise(keys[10], (N_SECTION, MH * HD, D), (MH * HD) ** -0.5, 0.15625, ((0, 2), (1, 4)))
    query_proj = noise(keys[11], (N_SECTION, D, AH * AD), D ** -0.5, 0.1875, ((0, 2), (2, 4)))
    keyval_proj = noise(keys[12], (N_SECTION, D, 2 * KVH * AD), D ** -0.5, 0.1875, ((0, 2),))
    output_proj = noise(keys[13], (N_SECTION, AH * AD, D), (AH * AD // 8) ** -0.5, 0.75, ((0, 2), (1, 4)))
    gate_up = noise(keys[14], (N_SECTION, 2, D, FF), D ** -0.5, 0.1875, ((0, 2), (3, 4)))
    down_proj = noise(keys[15], (N_SECTION, FF, D), FF ** -0.5, 0.125, ((0, 2), (1, 4)))
    return dict(inputs=inputs, cotangent=cotangent, segment_ids=segment_ids, norm_gains=norm_gains, mixer_in=mixer_in, state_proj=state_proj, step_proj=step_proj, conv_inner=conv_inner, conv_state=conv_state, head_params=head_params, mixer_out=mixer_out, query_proj=query_proj, keyval_proj=keyval_proj, output_proj=output_proj, gate_up=gate_up, down_proj=down_proj)


EPS = 1e-06
ROPE_BASE = 100000000000.0
NEG = -1e+30
HIGH = lax.Precision.HIGHEST

@jax.custom_vjp
def low(v):
    return lax.optimization_barrier(v.astype(jnp.bfloat16)).astype(jnp.float32)

@jax.custom_vjp
def low_back(v):
    return v

def low_keep(v):
    return (low(v), None)

def low_pass(kept, grad):
    return (grad,)

def back_keep(v):
    return (v, None)

def back_low(kept, grad):
    return (low(grad),)
low.defvjp(low_keep, low_pass)
low_back.defvjp(back_keep, back_low)

def rms_scale(row_values, gain_vec):
    return row_values * lax.rsqrt(lax.optimization_barrier(jnp.mean(row_values * row_values, axis=-1, keepdims=True)) + EPS) * gain_vec

def short_conv(values, weights, segment):
    length = values.shape[0]
    places = jnp.arange(length)
    running = jnp.zeros_like(values)
    for offset in range(weights.shape[0]):
        shifted = jnp.concatenate([jnp.zeros((offset, values.shape[1]), values.dtype), values[:length - offset]], axis=0)
        earlier = jnp.concatenate([jnp.full((offset,), -1, segment.dtype), segment[:length - offset]])
        same_doc = ((places >= offset) & (earlier == segment)).astype(values.dtype)
        running = running + weights[offset][None, :] * shifted * same_doc[:, None]
    return jax.nn.silu(running)

def ssd_weights(gram_matrix, step_raw, step_bias, decay_log, allowed):
    step_size = jax.nn.softplus(step_raw + step_bias)
    log_decay = -jnp.exp(decay_log) * step_size
    levels = jnp.cumsum(log_decay, axis=0).T
    spread = jnp.where(allowed[None], levels[:, :, None] - levels[:, None, :], NEG)
    return gram_matrix[None] * jnp.exp(spread) * step_size.T[:, None, :]

def rope_tables(length, head_width):
    half_width = head_width // 2
    frequency = ROPE_BASE ** (-(jnp.arange(half_width, dtype=jnp.float32) * 2.0 / head_width))
    angles = jnp.arange(length, dtype=jnp.float32)[:, None] * frequency[None, :]
    return (jnp.cos(angles)[:, None, :], jnp.sin(angles)[:, None, :])

def rotate(values, cosine, sine_table):
    half_width = values.shape[-1] // 2
    front_half = values[..., :half_width]
    back_half = values[..., half_width:]
    return jnp.concatenate([front_half * cosine - back_half * sine_table, back_half * cosine + front_half * sine_table], axis=-1)

def gate_mul(state_vals, gate_vals):
    return state_vals * jax.nn.silu(gate_vals)

def swiglu(gate_vals, up_vals):
    return jax.nn.silu(gate_vals) * up_vals

def head_group(normed, segment, allowed, cosine, sine_table, mixer_in, state_proj, step_proj, conv_inner, conv_state, head_params, mixer_out, query_proj, keyval_proj, output_proj):
    length = normed.shape[0]
    inner_width = mixer_in.shape[2]
    mamba_heads = inner_width // HD
    query_heads = query_proj.shape[1] // AD
    gate_input = low_back(jnp.einsum('sd,jdc->jsc', normed, mixer_in, precision=HIGH))
    state_input = low_back(jnp.einsum('sd,jdn->jsn', normed, state_proj, precision=HIGH))
    step_raw = low_back(jnp.dot(normed, step_proj, precision=HIGH))
    convolved = short_conv(jnp.concatenate([gate_input[1], state_input[0], state_input[1]], axis=-1), jnp.concatenate([conv_inner, conv_state[0], conv_state[1]], axis=-1), segment)
    x_conv = convolved[:, :inner_width]
    b_low = low(convolved[:, inner_width:inner_width + NS])
    c_low = low(convolved[:, inner_width + NS:])
    gram_matrix = low_back(jnp.dot(c_low, b_low.T, precision=HIGH))
    mix_weights = low(ssd_weights(gram_matrix, step_raw, head_params[0], head_params[1], allowed))
    x_heads = low(x_conv).reshape(length, mamba_heads, HD)
    state_out = jnp.einsum('hts,shp->thp', mix_weights, x_heads, precision=HIGH) + head_params[2][None, :, None] * x_conv.reshape(length, mamba_heads, HD)
    state_out = low_back(state_out.reshape(length, inner_width))
    gated = low(gate_mul(state_out, gate_input[0]))
    query = low_back(jnp.dot(normed, query_proj, precision=HIGH)).reshape(length, query_heads, AD)
    keyval = low_back(jnp.dot(normed, keyval_proj, precision=HIGH))
    q_low = low(rotate(query, cosine, sine_table))
    k_low = low(rotate(keyval[:, None, :AD], cosine, sine_table))[:, 0]
    v_low = low(keyval[:, AD:])
    scores = low_back(jnp.where(allowed[None], jnp.einsum('thd,sd->hts', q_low, k_low, precision=HIGH) * AD ** (-0.5), NEG))
    probs = low(jax.nn.softmax(scores, axis=-1))
    attended = low(low_back(jnp.einsum('hts,sd->thd', probs, v_low, precision=HIGH).reshape(length, query_heads * AD)))
    return jnp.dot(gated, mixer_out, precision=HIGH) + jnp.dot(attended, output_proj, precision=HIGH)

def layer(x_rows, segment, weights):
    norm_gains, mixer_in, state_proj, step_proj, conv_inner, conv_state, head_params, mixer_out, query_proj, keyval_proj, output_proj, gate_up, down_proj = weights
    length = x_rows.shape[0]
    groups = N_TENSOR
    places = jnp.arange(length)
    allowed = (segment[:, None] == segment[None, :]) & (places[:, None] >= places[None, :])
    cosine, sine_table = rope_tables(length, AD)
    normed = low(rms_scale(x_rows, norm_gains[0]))
    split_in = mixer_in.reshape(2, D, groups, -1).transpose(2, 0, 1, 3)
    split_step = step_proj.reshape(D, groups, -1).transpose(1, 0, 2)
    split_conv = conv_inner.reshape(KERNEL, groups, -1).transpose(1, 0, 2)
    split_heads = head_params.reshape(3, groups, -1).transpose(1, 0, 2)
    split_out = mixer_out.reshape(groups, -1, D)
    split_query = query_proj.reshape(D, groups, -1).transpose(1, 0, 2)
    keyval_heads = jnp.repeat(keyval_proj.reshape(D, 2, KVH, AD), groups // KVH, axis=2)
    split_keyval = keyval_heads.transpose(2, 0, 1, 3).reshape(groups, D, 2 * AD)
    split_output = output_proj.reshape(groups, -1, D)
    partial_out = jax.vmap(head_group, in_axes=(None, None, None, None, None, 0, None, 0, 0, None, 0, 0, 0, 0, 0))(normed, segment, allowed, cosine, sine_table, split_in, state_proj, split_step, split_conv, conv_state, split_heads, split_out, split_query, split_keyval, split_output)
    mixture = low_back(lax.optimization_barrier(jnp.sum(partial_out, axis=0)))
    resid = x_rows + mixture
    normed2 = low(rms_scale(resid, norm_gains[1]))
    gate_vals = low_back(jnp.einsum('sd,jdf->jsf', normed2, gate_up, precision=HIGH))
    hidden = low(swiglu(gate_vals[0], gate_vals[1]))
    return resid + low_back(jnp.dot(hidden, down_proj, precision=HIGH))

def reference(inputs, cotangent, segment_ids, norm_gains, mixer_in, state_proj, step_proj, conv_inner, conv_state, head_params, mixer_out, query_proj, keyval_proj, output_proj, gate_up, down_proj):
    weights = tuple((weight.astype(jnp.float32) for weight in (norm_gains, mixer_in, state_proj, step_proj, conv_inner, conv_state, head_params, mixer_out, query_proj, keyval_proj, output_proj, gate_up, down_proj)))
    sequences = MICRO * BATCH
    first_in = inputs.astype(jnp.float32).reshape(sequences, SEQ, D)
    segments = segment_ids.reshape(sequences, SEQ).astype(jnp.int32)
    probe = jnp.zeros_like(first_in)

    def model(start, probe_vals, params):
        lower = tuple((param[0] for param in params))
        upper = tuple((param[1] for param in params))

        def first_section(pair):
            return low(layer(pair[0], pair[1], lower))

        def second_section(pair):
            return layer(pair[0], pair[1], upper)
        middle = lax.map(jax.checkpoint(first_section), (start, segments))
        middle = low_back(middle + probe_vals)
        final = lax.map(jax.checkpoint(second_section), (middle, segments))
        return (middle, final)
    (middle, final), back = jax.vjp(model, first_in, probe, weights)
    d_start, d_middle, d_params = back((jnp.zeros_like(middle), cotangent.astype(jnp.float32).reshape(sequences, SEQ, D)))
    shape = (MICRO, BATCH, SEQ, D)
    section_outs = jnp.stack([middle.reshape(shape), final.reshape(shape)]).astype(jnp.bfloat16)
    section_grads = jnp.stack([d_start.reshape(shape), d_middle.reshape(shape)]).astype(jnp.bfloat16)
    return (section_outs, section_grads, d_params[0], d_params[1], d_params[2], d_params[3], d_params[4], d_params[5], d_params[6], d_params[7], d_params[8], d_params[9], d_params[10], d_params[11], d_params[12])
```

```python
import functools

import jax
import jax.numpy as jnp
import numpy as np
from jax import lax
from jax.experimental import pallas as pl
from jax.experimental.pallas import tpu as pltpu
from jax.sharding import PartitionSpec as P

HD = 64
NS = 128
AH = 8
KVH = 2
AD = 64
TAPS = 4
PAD = 128

EPS = 1e-06
ROPE_BASE = 100000000000.0
NEG = -1e30

F32 = jnp.float32
BF16 = jnp.bfloat16
HIGH = lax.Precision.HIGHEST
MIB = 1024 * 1024

CORE = [(i, i ^ 1) for i in range(4)]
FAR = [(i, i ^ 2) for i in range(4)]


def dot_nn(a, b, precision=None):
    return lax.dot_general(
        a, b, (((1,), (0,)), ((), ())), preferred_element_type=F32, precision=precision
    )


def dot_nt(a, b):
    return lax.dot_general(a, b, (((1,), (1,)), ((), ())), preferred_element_type=F32)


def dot_tn(a, b):
    return lax.dot_general(a, b, (((0,), (0,)), ((), ())), preferred_element_type=F32)


def sigmoid(a):
    return 1.0 / (1.0 + jnp.exp(-a))


def silu_slope(a, s):
    return s * (1.0 + a * (1.0 - s))


def assemble(t, dst, pieces):
    own, far, core, both = pieces
    dst[t] = own[...]
    dst[t ^ 2] = far[...]
    dst[t ^ 1] = core[...]
    dst[t ^ 3] = both[...]


def rows_of(ref):
    blocks, rows, width = ref.shape
    return ref[...].reshape(blocks * rows, width)


def give_parts(t, full, scr, keep_ref, send_ref):
    scr[...] = full.astype(BF16).reshape(scr.shape)
    keep_ref[0] = scr[t]
    keep_ref[1] = scr[t ^ 2]
    send_ref[0] = scr[t ^ 1]
    send_ref[1] = scr[t ^ 3]


def lane_parity(rows, width=128):
    return lax.broadcasted_iota(jnp.int32, (rows, width), 1)


def partner(a):
    lane = lax.broadcasted_iota(jnp.int32, a.shape, 1)
    return jnp.where((lane & 32) == 0, pltpu.roll(a, 96, 1), pltpu.roll(a, 32, 1))


def shift_down(a, k):
    return a if k == 0 else pltpu.roll(a, k, 0)


def shift_up(a, k):
    return a if k == 0 else pltpu.roll(a, a.shape[0] - k, 0)


def mixer_front(xs, gain_ref, wcat, taps, heads, segc, segr, tables):
    length = xs.shape[0]
    inner = taps.shape[1] - 2 * NS
    r = lax.rsqrt(jnp.mean(xs * xs, axis=-1, keepdims=True) + EPS)
    normed = (xs * r * gain_ref[0:1, :]).astype(BF16)
    proj = dot_nn(normed, wcat[...])
    z = proj[:, :inner]
    v = proj[:, inner : 2 * inner + 2 * NS]
    seg = segc[...]
    place = lax.broadcasted_iota(jnp.int32, (length, 1), 0)
    keeps = []
    for k in range(TAPS):
        earlier = shift_down(seg, k)
        same = (place >= k) & (earlier[:, 0:1] == seg[:, 0:1])
        keeps.append(jnp.where(same, 1.0, 0.0))
    pre = taps[0:1, :] * v
    for k in range(1, TAPS):
        pre = pre + taps[k : k + 1, :] * (shift_down(v, k) * keeps[k])
    psig = sigmoid(pre)
    conv = pre * psig
    xc = conv[:, :inner]
    b_low = conv[:, inner : inner + NS].astype(BF16)
    c_low = conv[:, inner + NS :].astype(BF16)
    gram = dot_nt(c_low, b_low)
    base = 2 * inner + 2 * NS
    q_raw = proj[:, base : base + 128]
    kv_raw = proj[:, base + 128 : base + 256]
    step_cols = proj[:, base + 256 :]
    raw = jnp.transpose(step_cols)[:8] + heads[:, 0:1]
    step = jnp.maximum(raw, 0.0) + jnp.log1p(jnp.exp(-jnp.abs(raw)))
    rate = jnp.exp(heads[:, 1:2])
    row = lax.broadcasted_iota(jnp.int32, (length, length), 0)
    col = lax.broadcasted_iota(jnp.int32, (length, length), 1)
    upper = jnp.where(row <= col, 1.0, 0.0)
    level = dot_nn(-rate * step, upper, HIGH)
    level_cols = jnp.transpose(
        jnp.concatenate([level, jnp.zeros((PAD - 8, length), F32)], axis=0)
    )
    allowed = (row >= col) & (segc[:, 0:1] == segr[0:1, :])
    cos_q, sin_q, cos_kv, sin_kv = tables[0], tables[1], tables[2], tables[3]
    q_rot = q_raw * cos_q + partner(q_raw) * sin_q
    kv_rot = kv_raw * cos_kv + partner(kv_raw) * sin_kv
    q01 = q_rot.astype(BF16)
    q10 = pltpu.roll(q_rot, 64, 1).astype(BF16)
    kv = kv_rot.astype(BF16)
    vk = pltpu.roll(kv_rot, 64, 1).astype(BF16)
    lane = lane_parity(length)
    low_half = lane < 64
    zero = jnp.zeros((length, 128), BF16)

    def lo(a):
        return jnp.where(low_half, a, zero)

    def hi(a):
        return jnp.where(low_half, zero, a)

    return dict(
        normed=normed, z=z, v=v, keeps=keeps, pre=pre, psig=psig, xc=xc, b_low=b_low,
        c_low=c_low, gram=gram, raw=raw, step=step, rate=rate, level=level,
        level_cols=level_cols, allowed=allowed, q01=q01, q10=q10, kv=kv, vk=vk, lo=lo,
        hi=hi, inner=inner, length=length, row=row, col=col,
    )


def decay_of(f, h):
    diff = f["level_cols"][:, h : h + 1] - f["level"][h : h + 1, :]
    return jnp.exp(jnp.where(f["allowed"], diff, NEG))


def probs_of(f, h):
    lo, hi = f["lo"], f["hi"]
    qh = f["q01"] if h == 0 else f["q10"]
    scores = jnp.where(f["allowed"], dot_nt(lo(qh), f["kv"]) * (AD ** (-0.5)), NEG)
    peak = jnp.max(scores, axis=-1, keepdims=True)
    powers = jnp.exp(scores - peak)
    return powers / jnp.sum(powers, axis=-1, keepdims=True)


def mixer_fwd_kernel(
    t_ref, own, far, core, both, gain, wcat, wout, taps, heads, segc, segr, tables,
    keep_ref, send_ref, x_scr, act, out_scr,
):
    t = t_ref[0]
    assemble(t, x_scr, (own, far, core, both))
    f = mixer_front(rows_of(x_scr).astype(F32), gain, wcat, taps, heads, segc, segr, tables)
    lo, hi, inner = f["lo"], f["hi"], f["inner"]
    for p in range(inner // 128):
        cs = slice(128 * p, 128 * p + 128)
        xp = f["xc"][:, cs]
        xl = xp.astype(BF16)
        y = taps[4:5, cs] * xp
        for j, half in enumerate((lo, hi)):
            h = 2 * p + j
            w = f["gram"] * decay_of(f, h) * f["step"][h : h + 1, :]
            y = y + dot_nn(w.astype(BF16), half(xl))
        z = f["z"][:, cs]
        act[:, cs] = (y * (z * sigmoid(z))).astype(BF16)
    att = dot_nn(probs_of(f, 0).astype(BF16), lo(f["vk"]))
    att = att + dot_nn(probs_of(f, 1).astype(BF16), hi(f["kv"]))
    act[:, inner : inner + 128] = att.astype(BF16)
    give_parts(t, dot_nn(act[...], wout[...]), out_scr, keep_ref, send_ref)


def mixer_bwd_kernel(
    t_ref, own, far, core, both, g_own, g_far, g_core, g_both, gain, wcat, wout, taps, heads,
    segc, segr, tables,
    keep_ref, send_ref, normed_ref, dy, act, dm_ref, small_ref, headg_ref,
    x_scr, dm_scr, out_scr,
):
    t = t_ref[0]
    assemble(t, x_scr, (own, far, core, both))
    assemble(t, dm_scr, (g_own, g_far, g_core, g_both))
    f = mixer_front(rows_of(x_scr).astype(F32), gain, wcat, taps, heads, segc, segr, tables)
    lo, hi, inner, length = f["lo"], f["hi"], f["inner"], f["length"]
    normed_ref[...] = f["normed"]
    dm = rows_of(dm_scr)
    dm_ref[...] = dm
    dact = dot_nt(dm, wout[...])
    gram, step, rate = f["gram"], f["step"], f["rate"]
    lane = lax.broadcasted_iota(jnp.int32, (length, PAD), 1)
    sub = lax.broadcasted_iota(jnp.int32, (8, length), 0)
    d_gram = jnp.zeros((length, length), F32)
    row_sums = jnp.zeros((length, PAD), F32)
    d_step = jnp.zeros((8, length), F32)
    small_ref[...] = jnp.zeros_like(small_ref)
    d_parts = []
    for p in range(inner // 128):
        cs = slice(128 * p, 128 * p + 128)
        xp = f["xc"][:, cs]
        xl = xp.astype(BF16)
        z = f["z"][:, cs]
        zs = sigmoid(z)
        dg = dact[:, cs]
        ds_low = (dg * (z * zs)).astype(BF16)
        ds = ds_low.astype(F32)
        skip = taps[4:5, cs]
        y = skip * xp
        dxc = skip * ds
        for j, half in enumerate((lo, hi)):
            h = 2 * p + j
            e = decay_of(f, h)
            step_h = step[h : h + 1, :]
            w_low = (gram * e * step_h).astype(BF16)
            ds_h = half(ds_low)
            y = y + dot_nn(w_low, half(xl))
            dxc = dxc + dot_tn(w_low, ds_h)
            te = dot_nt(ds_h, xl) * e
            d_gram = d_gram + te * step_h
            tg = te * gram
            d_step = jnp.where(sub == h, jnp.sum(tg, axis=0, keepdims=True), d_step)
            row_sums = jnp.where(
                lane == h, jnp.sum(tg * step_h, axis=1, keepdims=True), row_sums
            )
        act[:, cs] = (y * (z * zs)).astype(BF16)
        dy[:, cs] = (dg * y * silu_slope(z, zs)).astype(BF16)
        small_ref[4:5, cs] = jnp.sum(ds * xp, axis=0, keepdims=True)
        d_parts.append(dxc)
    d_level = jnp.transpose(row_sums)[:8] - step * d_step
    later = jnp.where(f["row"] >= f["col"], 1.0, 0.0)
    tail = dot_nn(d_level, later, HIGH)
    d_step = d_step - rate * tail
    d_raw = d_step * sigmoid(f["raw"])
    d_decay = -rate * jnp.sum(step * tail, axis=1, keepdims=True)
    d_bias = jnp.sum(d_raw, axis=1, keepdims=True)
    lane8 = lax.broadcasted_iota(jnp.int32, (8, PAD), 1)
    headg_ref[...] = jnp.where(lane8 == 0, d_bias, jnp.where(lane8 == 1, d_decay, 0.0))
    base = 2 * inner + 2 * NS
    dy[:, base + 256 : base + 384] = jnp.transpose(
        jnp.concatenate([d_raw, jnp.zeros((PAD - 8, length), F32)], axis=0)
    ).astype(BF16)
    dg_low = d_gram.astype(BF16)
    d_parts.append(dot_tn(dg_low, f["c_low"]))
    d_parts.append(dot_nn(dg_low, f["b_low"]))
    for p, part in enumerate(d_parts):
        cs = slice(128 * p, 128 * p + 128)
        dp = part * silu_slope(f["pre"][:, cs], f["psig"][:, cs])
        v = f["v"][:, cs]
        dv = taps[0:1, cs] * dp
        small_ref[0:1, cs] = jnp.sum(dp * v, axis=0, keepdims=True)
        for k in range(1, TAPS):
            kept = dp * f["keeps"][k]
            dv = dv + taps[k : k + 1, cs] * shift_up(kept, k)
            small_ref[k : k + 1, cs] = jnp.sum(kept * shift_down(v, k), axis=0, keepdims=True)
        dy[:, inner + 128 * p : inner + 128 * p + 128] = dv.astype(BF16)
    da01f = dact[:, inner : inner + 128]
    da01 = da01f.astype(BF16)
    da10 = pltpu.roll(da01f, 64, 1).astype(BF16)
    p0 = probs_of(f, 0)
    p1 = probs_of(f, 1)
    p0l, p1l = p0.astype(BF16), p1.astype(BF16)
    att = dot_nn(p0l, lo(f["vk"])) + dot_nn(p1l, hi(f["kv"]))
    act[:, inner : inner + 128] = att.astype(BF16)
    d_value = dot_tn(p0l, hi(da10)) + dot_tn(p1l, hi(da01))
    dp0 = dot_nt(lo(da01), f["vk"])
    dp1 = dot_nt(hi(da01), f["kv"])
    ds0 = (p0 * (dp0 - jnp.sum(p0 * dp0, axis=-1, keepdims=True))).astype(BF16)
    ds1 = (p1 * (dp1 - jnp.sum(p1 * dp1, axis=-1, keepdims=True))).astype(BF16)
    scale = AD ** (-0.5)
    dq = (dot_nn(ds0, lo(f["kv"])) + dot_nn(ds1, hi(f["vk"]))) * scale
    dkv = (dot_tn(ds0, lo(f["q01"])) + dot_tn(ds1, lo(f["q10"]))) * scale + d_value
    cos_q, sin_q, cos_kv, sin_kv = tables[0], tables[1], tables[2], tables[3]
    dy[:, base : base + 128] = (dq * cos_q - partner(dq) * sin_q).astype(BF16)
    dy[:, base + 128 : base + 256] = (dkv * cos_kv - partner(dkv) * sin_kv).astype(BF16)
    give_parts(t, dot_nt(dy[...], wcat[...]), out_scr, keep_ref, send_ref)


def ffn_fwd_kernel(
    t_ref, own, far, core, both, wgu, wd, keep_ref, send_ref, n_scr, out_scr
):
    t = t_ref[0]
    assemble(t, n_scr, (own, far, core, both))
    n2 = rows_of(n_scr)
    g = dot_nn(n2, wgu[0])
    u = dot_nn(n2, wgu[1])
    hidden = (g * sigmoid(g) * u).astype(BF16)
    give_parts(t, dot_nn(hidden, wd[...]), out_scr, keep_ref, send_ref)


def ffn_bwd_kernel(
    t_ref, own, far, core, both, g_own, g_far, g_core, g_both, wgu, wd,
    keep_ref, send_ref, n_ref, dgu, hid_ref, go_ref, n_scr, go_scr, out_scr,
):
    t = t_ref[0]
    assemble(t, n_scr, (own, far, core, both))
    assemble(t, go_scr, (g_own, g_far, g_core, g_both))
    n2 = rows_of(n_scr)
    go = rows_of(go_scr)
    n_ref[...] = n2
    go_ref[...] = go
    width = wd.shape[0]
    g = dot_nn(n2, wgu[0])
    u = dot_nn(n2, wgu[1])
    dh = dot_nt(go, wd[...])
    s = sigmoid(g)
    act = g * s
    hid_ref[...] = (act * u).astype(BF16)
    dg = (dh * u * silu_slope(g, s)).astype(BF16)
    du = (dh * act).astype(BF16)
    dgu[:, :width] = dg
    dgu[:, width:] = du
    give_parts(t, dot_nt(dg, wgu[0]) + dot_nt(du, wgu[1]), out_scr, keep_ref, send_ref)


def resid_norm_kernel(x, keep, recv, last, gain, resid_ref, n_ref):
    a = x[...].astype(F32) + (
        keep[0].astype(F32) + recv[0].astype(F32) + last[...].astype(F32)
    )
    resid_ref[...] = a
    r = lax.rsqrt(jnp.mean(a * a, axis=-1, keepdims=True) + EPS)
    n_ref[...] = (a * r * gain[...]).astype(BF16)


def norm_bwd_kernel(a_ref, keep, recv, last, gain, base, d_ref, low_ref, dgain_ref):
    a = a_ref[...].astype(F32)
    dn = keep[0].astype(F32) + recv[0].astype(F32) + last[...].astype(F32)
    r = lax.rsqrt(jnp.mean(a * a, axis=-1, keepdims=True) + EPS)
    dgain_ref[...] = jnp.sum(dn * a * r, axis=0, keepdims=True)
    dng = dn * gain[...]
    inner = jnp.mean(dng * a, axis=-1, keepdims=True)
    d = base[...].astype(F32) + (r * dng - a * (r * r * r) * inner)
    d_ref[...] = d
    low_ref[...] = d.astype(BF16)


def wgrad_ffn_kernel(na, nb, ga, gb, dgua, dgub, ha, hb, out):
    width = dgua.shape[1]
    out[:, :width] = (dot_tn(na[...], dgua[...]) + dot_tn(nb[...], dgub[...])).astype(BF16)
    out[:, width:] = (dot_tn(ga[...], ha[...]) + dot_tn(gb[...], hb[...])).astype(BF16)


def wgrad_mix_kernel(inner, na, nb, ga, gb, dya, dyb, aa, ab, out, shared):
    zu = 2 * inner
    bc = zu + 2 * NS
    full = dot_tn(na[...], dya[...]) + dot_tn(nb[...], dyb[...])
    full = full.astype(BF16)
    out[:, :zu] = full[:, :zu]
    out[:, zu : zu + 128] = full[:, bc : bc + 128]
    out[:, zu + 128 : zu + 256] = full[:, bc + 256 :]
    out[:, zu + 256 :] = (dot_tn(ga[...], aa[...]) + dot_tn(gb[...], ab[...])).astype(BF16)
    shared[:, : 2 * NS] = full[:, zu:bc]
    shared[:, 2 * NS :] = full[:, bc + 128 : bc + 256]


VM = pl.BlockSpec(memory_space=pltpu.VMEM)
SM = pl.BlockSpec(memory_space=pltpu.SMEM)


def sds(shape, dtype):
    return jax.ShapeDtypeStruct(tuple(shape), dtype)


def params(mib):
    return pltpu.CompilerParams(vmem_limit_bytes=mib * MIB)


def cost(flops, nbytes, trans=0):
    return pl.CostEstimate(flops=int(flops), bytes_accessed=int(nbytes), transcendentals=int(trans))


def mixer_fwd(t, pieces, w, seg):
    rows, width = pieces[0].shape
    wcat, wout = w["wcat"], w["wout"]
    length = 4 * rows
    return pl.pallas_call(
        mixer_fwd_kernel,
        out_shape=[sds((2, rows, width), BF16)] * 2,
        in_specs=[SM] + [VM] * 12,
        out_specs=[VM] * 2,
        scratch_shapes=[
            pltpu.VMEM((4, rows, width), BF16),
            pltpu.VMEM((length, wout.shape[0]), BF16),
            pltpu.VMEM((4, rows, width), BF16),
        ],
        compiler_params=params(32),
        cost_estimate=cost(2 * length * (wcat.size + wout.size) * 2, 2 * (wcat.size + wout.size)),
        name="mixer_fwd",
    )(t, *pieces, w["gain"], wcat, wout, w["taps"], w["heads"], *seg, w["tables"])


def mixer_bwd(t, pieces, grads, w, seg):
    rows, width = pieces[0].shape
    wcat, wout = w["wcat"], w["wout"]
    length = 4 * rows
    return pl.pallas_call(
        mixer_bwd_kernel,
        out_shape=[
            sds((2, rows, width), BF16),
            sds((2, rows, width), BF16),
            sds((length, width), BF16),
            sds((length, wcat.shape[1]), BF16),
            sds((length, wout.shape[0]), BF16),
            sds((length, width), BF16),
            sds((8, w["taps"].shape[1]), F32),
            sds((8, PAD), F32),
        ],
        in_specs=[SM] + [VM] * 16,
        out_specs=[VM] * 8,
        scratch_shapes=[pltpu.VMEM((4, rows, width), BF16)] * 3,
        compiler_params=params(40),
        cost_estimate=cost(2 * length * (wcat.size + wout.size) * 5, 2 * (wcat.size + wout.size)),
        name="mixer_bwd",
    )(t, *pieces, *grads, w["gain"], wcat, wout, w["taps"], w["heads"], *seg, w["tables"])


def ffn_fwd(t, pieces, w):
    rows, width = pieces[0].shape
    wgu, wd = w["wgu"], w["wd"]
    return pl.pallas_call(
        ffn_fwd_kernel,
        out_shape=[sds((2, rows, width), BF16)] * 2,
        in_specs=[SM] + [VM] * 6,
        out_specs=[VM] * 2,
        scratch_shapes=[pltpu.VMEM((4, rows, width), BF16)] * 2,
        compiler_params=params(24),
        cost_estimate=cost(8 * rows * (wgu.size + wd.size), 2 * (wgu.size + wd.size)),
        name="ffn_fwd",
    )(t, *pieces, wgu, wd)


def ffn_bwd(t, pieces, grads, w):
    rows, width = pieces[0].shape
    wgu, wd = w["wgu"], w["wd"]
    length, units = 4 * rows, wd.shape[0]
    return pl.pallas_call(
        ffn_bwd_kernel,
        out_shape=[
            sds((2, rows, width), BF16),
            sds((2, rows, width), BF16),
            sds((length, width), BF16),
            sds((length, 2 * units), BF16),
            sds((length, units), BF16),
            sds((length, width), BF16),
        ],
        in_specs=[SM] + [VM] * 10,
        out_specs=[VM] * 6,
        scratch_shapes=[pltpu.VMEM((4, rows, width), BF16)] * 3,
        compiler_params=params(24),
        cost_estimate=cost(16 * rows * (wgu.size + wd.size), 2 * (wgu.size + wd.size)),
        name="ffn_bwd",
    )(t, *pieces, *grads, wgu, wd)


def first_block(rows, width):
    return pl.BlockSpec((1, rows, width), lambda i: (0, 0, 0))


def whole_block(shape):
    return pl.BlockSpec(shape, lambda i: (0,) * len(shape))


def resid_norm(x, part, gain):
    rows, width = x.shape
    flat = whole_block((rows, width))
    return pl.pallas_call(
        resid_norm_kernel,
        grid=(1,),
        out_shape=[sds((rows, width), F32), sds((rows, width), BF16)],
        in_specs=[flat, first_block(rows, width), first_block(rows, width), flat]
        + [whole_block((1, width))],
        out_specs=[flat, flat],
        cost_estimate=cost(10 * rows * width, 12 * rows * width),
        name="resid_norm",
    )(x, *part, gain)


def norm_bwd(a, part, gain, base):
    rows, width = a.shape
    flat = whole_block((rows, width))
    return pl.pallas_call(
        norm_bwd_kernel,
        grid=(1,),
        out_shape=[sds((rows, width), F32), sds((rows, width), BF16), sds((1, width), F32)],
        in_specs=[flat, first_block(rows, width), first_block(rows, width), flat]
        + [whole_block((1, width)), flat],
        out_specs=[flat, flat, whole_block((1, width))],
        cost_estimate=cost(20 * rows * width, 16 * rows * width),
        name="norm_bwd",
    )(a, *part, gain, base)


def wgrad_ffn(saved):
    (na, ga, dgua, ha), (nb, gb, dgub, hb) = saved
    length, width = na.shape
    cols = dgua.shape[1] + ha.shape[1]
    block = pl.BlockSpec((length, 256), lambda i: (0, i))
    return pl.pallas_call(
        wgrad_ffn_kernel,
        grid=(width // 256,),
        out_shape=sds((width, cols), BF16),
        in_specs=[block] * 4 + [whole_block(dgua.shape)] * 2 + [whole_block(ha.shape)] * 2,
        out_specs=pl.BlockSpec((256, cols), lambda i: (i, 0)),
        compiler_params=params(24),
        cost_estimate=cost(4 * length * width * cols, 2 * width * cols),
        name="wgrad_ffn",
    )(na, nb, ga, gb, dgua, dgub, ha, hb)


def wgrad_mix(saved, inner):
    (na, ga, dya, aa), (nb, gb, dyb, ab) = saved
    length, width = na.shape
    cols = 2 * inner + 256 + aa.shape[1]
    block = pl.BlockSpec((length, 256), lambda i: (0, i))
    return pl.pallas_call(
        functools.partial(wgrad_mix_kernel, inner),
        grid=(width // 256,),
        out_shape=[sds((width, cols), BF16), sds((width, 2 * NS + 128), BF16)],
        in_specs=[block] * 4 + [whole_block(dya.shape)] * 2 + [whole_block(aa.shape)] * 2,
        out_specs=[
            pl.BlockSpec((256, cols), lambda i: (i, 0)),
            pl.BlockSpec((256, 2 * NS + 128), lambda i: (i, 0)),
        ],
        compiler_params=params(24),
        cost_estimate=cost(4 * length * width * (cols + 384), 2 * width * (cols + 384)),
        name="wgrad_mix",
    )(na, nb, ga, gb, dya, dyb, aa, ab)


def gather(own):
    far = lax.ppermute(own, "tensor", FAR)
    core = lax.ppermute(own, "tensor", CORE)
    both = lax.ppermute(far, "tensor", CORE)
    return (own, far, core, both)


def scatter(keep, send):
    recv = lax.ppermute(send, "tensor", CORE)
    pair = (keep[1].astype(F32) + recv[1].astype(F32)).astype(BF16)
    last = lax.ppermute(pair, "tensor", FAR)
    return (keep, recv, last)


def rope_tables(length):
    half = AD // 2
    freq = np.float32(ROPE_BASE) ** (
        -(np.arange(half, dtype=np.float32) * np.float32(2.0) / np.float32(AD))
    )
    angles = np.arange(length, dtype=np.float32)[:, None] * freq[None, :].astype(np.float32)
    cos = np.cos(angles).astype(np.float32)
    sin = np.sin(angles).astype(np.float32)
    cos_h = np.concatenate([cos, cos], axis=1)
    sin_h = np.concatenate([-sin, sin], axis=1)
    one, zero = np.ones_like(cos_h), np.zeros_like(sin_h)
    return np.stack(
        [
            np.concatenate([cos_h, cos_h], axis=1),
            np.concatenate([sin_h, sin_h], axis=1),
            np.concatenate([cos_h, one], axis=1),
            np.concatenate([sin_h, zero], axis=1),
        ]
    )


def per_device(
    inputs,
    cotangent,
    segment_ids,
    norm_gains,
    mixer_in,
    state_proj,
    step_proj,
    conv_inner,
    conv_state,
    head_params,
    mixer_out,
    query_proj,
    keyval_proj,
    output_proj,
    gate_up,
    down_proj,
):
    section_now = lax.axis_index("section")
    tensor_now = lax.axis_index("tensor")
    dp_count = lax.axis_size("dp")
    tensor_count = lax.axis_size("tensor")
    micro_count = inputs.shape[0]
    width = inputs.shape[3]
    length = segment_ids.shape[2]
    inner = mixer_in.shape[3]
    heads_here = inner // HD
    units = down_proj.shape[1]
    micros = range(micro_count)

    t = tensor_now.reshape(1).astype(jnp.int32)
    gains = norm_gains[0].astype(F32)
    query_heads = query_proj.shape[2] // AD
    key_group = tensor_now * query_heads // (AH // KVH)
    keyval_all = keyval_proj[0].reshape(width, 2, KVH, AD)
    keyval_here = lax.dynamic_index_in_dim(keyval_all, key_group, 2, keepdims=False).reshape(
        width, 2 * AD
    )
    wcat = jnp.concatenate(
        [
            mixer_in[0, 0],
            mixer_in[0, 1],
            state_proj[0, 0],
            state_proj[0, 1],
            query_proj[0],
            keyval_here,
            jnp.pad(step_proj[0], ((0, 0), (0, PAD - heads_here))),
        ],
        axis=1,
    )
    taps = jnp.concatenate([conv_inner[0], conv_state[0, 0], conv_state[0, 1]], axis=-1).astype(F32)
    skip = jnp.repeat(head_params[0, 2], HD)
    taps = jnp.concatenate(
        [taps, jnp.pad(skip, (0, 2 * NS))[None], jnp.zeros((3, inner + 2 * NS), F32)], axis=0
    )
    heads = jnp.pad(head_params[0].T, ((0, 8 - heads_here), (0, PAD - 3)))
    weights = dict(
        gain=gains[0:1],
        wcat=wcat,
        wout=jnp.concatenate([mixer_out[0], output_proj[0]], axis=0),
        taps=taps,
        heads=heads,
        tables=jnp.asarray(rope_tables(length)),
        wgu=gate_up[0],
        wd=down_proj[0],
    )
    gain2 = gains[1:2]
    segs = [
        (
            jnp.broadcast_to(segment_ids[m, 0][:, None], (length, PAD)),
            jnp.broadcast_to(segment_ids[m, 0][None, :], (8, length)),
        )
        for m in micros
    ]

    def forward(x_own):
        pieces = [gather(x_own[m]) for m in micros]
        parts = [scatter(*mixer_fwd(t, pieces[m], weights, segs[m])) for m in micros]
        resid, n2 = zip(*[resid_norm(x_own[m], parts[m], gain2) for m in micros])
        n_pieces = [gather(n2[m]) for m in micros]
        outs = [scatter(*ffn_fwd(t, n_pieces[m], weights)) for m in micros]
        result = [
            (
                resid[m]
                + (
                    outs[m][0][0].astype(F32)
                    + outs[m][1][0].astype(F32)
                    + outs[m][2].astype(F32)
                )
            ).astype(BF16)
            for m in micros
        ]
        return result, pieces, n_pieces, resid

    def backward(go, saved, x_own):
        pieces, n_pieces, resid = saved
        g_pieces = [gather(go[m]) for m in micros]
        ffn = [ffn_bwd(t, n_pieces[m], g_pieces[m], weights) for m in micros]
        parts = [scatter(ffn[m][0], ffn[m][1]) for m in micros]
        mid = [norm_bwd(resid[m], parts[m], gain2, go[m]) for m in micros]
        d_pieces = [gather(mid[m][1]) for m in micros]
        mix = [mixer_bwd(t, pieces[m], d_pieces[m], weights, segs[m]) for m in micros]
        parts1 = [scatter(mix[m][0], mix[m][1]) for m in micros]
        low = [norm_bwd(x_own[m], parts1[m], gains[0:1], mid[m][0]) for m in micros]
        return [low[m][1] for m in micros], ffn, mix, mid, low

    first = [inputs[m, 0] for m in micros]
    top = [cotangent[m, 0] for m in micros]

    out0, _, _, _ = forward(first)
    received = [lax.ppermute(out0[m], "section", [(0, 1)]) for m in micros]
    x_own = [jnp.where(section_now == 0, first[m], received[m]) for m in micros]
    out1, pieces, n_pieces, resid = forward(x_own)
    saved = (pieces, n_pieces, resid)
    grad1, _, _, _, _ = backward(top, saved, x_own)
    grad_in = [lax.ppermute(grad1[m], "section", [(1, 0)]) for m in micros]
    go = [jnp.where(section_now == 1, top[m], grad_in[m]) for m in micros]
    d_low, ffn, mix, mid, low = backward(go, saved, x_own)

    g_ffn = wgrad_ffn([(ffn[m][2], ffn[m][5], ffn[m][3], ffn[m][4]) for m in micros])
    r_ffn = lax.psum_scatter(g_ffn, "dp", scatter_dimension=0, tiled=True)
    g_mix, g_shared = wgrad_mix(
        [(mix[m][2], mix[m][5], mix[m][3], mix[m][4]) for m in micros], inner
    )
    r_mix = lax.psum_scatter(g_mix, "dp", scatter_dimension=0, tiled=True)

    rows16 = width // (dp_count * tensor_count)
    keyval_g = g_shared[:, 2 * NS :].reshape(width, 2, 1, AD)
    selector = (jnp.arange(KVH) == key_group)[None, None, :, None]
    keyval_g = jnp.where(selector, keyval_g, jnp.zeros((), BF16)).reshape(width, 2 * KVH * AD)
    shared = jnp.concatenate([g_shared[:, : 2 * NS], keyval_g], axis=1)
    shared_cols = shared.shape[1]
    shared = (
        shared.reshape(dp_count, tensor_count, rows16, shared_cols)
        .transpose(1, 0, 2, 3)
        .reshape(tensor_count, dp_count * rows16, shared_cols)
    )

    def block(flip):
        return lax.dynamic_index_in_dim(shared, tensor_now ^ flip, 0, keepdims=False)

    keep, recv, last = scatter(
        jnp.stack([block(0), block(2)]), jnp.stack([block(1), block(3)])
    )
    shared_sum = (keep[0].astype(F32) + recv[0].astype(F32) + last.astype(F32)).astype(BF16)
    r_shared = lax.psum_scatter(shared_sum, "dp", scatter_dimension=0, tiled=True).astype(F32)

    small = sum(mix[m][6] for m in micros)
    headg = sum(mix[m][7] for m in micros)
    d_skip = small[4, :inner].reshape(heads_here, HD).sum(axis=1)
    over_all = jnp.concatenate(
        [
            sum(low[m][2] for m in micros)[0],
            sum(mid[m][2] for m in micros)[0],
            small[:TAPS, inner:].reshape(-1),
        ]
    )
    per_head = jnp.concatenate(
        [
            small[:TAPS, :inner].reshape(-1),
            headg[:heads_here, 0],
            headg[:heads_here, 1],
            d_skip,
        ]
    )
    split_at = over_all.shape[0]
    vector = jnp.concatenate([over_all, per_head])
    bit = 1
    while bit < dp_count:
        vector = vector + lax.ppermute(vector, "dp", [(i, i ^ bit) for i in range(dp_count)])
        bit *= 2
    over_all, per_head = vector[:split_at], vector[split_at:]
    over_all = over_all + lax.ppermute(over_all, "tensor", CORE)
    over_all = over_all + lax.ppermute(over_all, "tensor", FAR)
    place = lax.axis_index("dp") * tensor_count + tensor_now
    pick = functools.partial(lax.dynamic_slice_in_dim, axis=1)
    grad_gains = pick(over_all[: 2 * width].reshape(2, width), place * rows16, rows16)
    state_taps = over_all[2 * width :].reshape(TAPS, 2, NS).transpose(1, 0, 2)
    each = NS // (dp_count * tensor_count)
    grad_conv_state = lax.dynamic_slice_in_dim(state_taps, place * each, each, axis=2)
    grad_conv_inner = per_head[: TAPS * inner].reshape(TAPS, inner)
    grad_heads = per_head[TAPS * inner :].reshape(3, heads_here)

    r_ffn = r_ffn.astype(F32)
    r_mix = r_mix.astype(F32)
    grad_gate_up = jnp.stack([r_ffn[:, :units], r_ffn[:, units : 2 * units]])
    grad_down = r_ffn[:, 2 * units :].T
    grad_mixer_in = jnp.stack([r_mix[:, :inner], r_mix[:, inner : 2 * inner]])
    base = 2 * inner
    grad_query = r_mix[:, base : base + 128]
    grad_step = r_mix[:, base + 128 : base + 128 + heads_here]
    outs_t = r_mix[:, base + 256 :].T
    grad_mixer_out = outs_t[:inner]
    grad_output = outs_t[inner:]
    grad_state = jnp.stack([r_shared[:, :NS], r_shared[:, NS : 2 * NS]])
    grad_keyval = r_shared[:, 2 * NS :]
    return (
        jnp.stack(out1)[None, :, None],
        jnp.stack(d_low)[None, :, None],
        grad_gains[None],
        grad_mixer_in[None],
        grad_state[None],
        grad_step[None],
        grad_conv_inner[None],
        grad_conv_state[None],
        grad_heads[None],
        grad_mixer_out[None],
        grad_query[None],
        grad_keyval[None],
        grad_output[None],
        grad_gate_up[None],
        grad_down[None],
    )


def solution(mesh):
    placed = (
        P(None, "dp", "tensor", None),
        P(None, "dp", "tensor", None),
        P(None, "dp", None),
        P("section", None, None),
        P("section", None, None, "tensor"),
        P("section", None, None, None),
        P("section", None, "tensor"),
        P("section", None, "tensor"),
        P("section", None, None, None),
        P("section", None, "tensor"),
        P("section", "tensor", None),
        P("section", None, "tensor"),
        P("section", None, None),
        P("section", "tensor", None),
        P("section", None, None, "tensor"),
        P("section", "tensor", None),
    )
    return jax.shard_map(
        per_device,
        mesh=mesh,
        in_specs=placed,
        out_specs=(
            P("section", None, "dp", "tensor", None),
            P("section", None, "dp", "tensor", None),
            P("section", None, ("dp", "tensor")),
            P("section", None, "dp", "tensor"),
            P("section", None, ("dp", "tensor"), None),
            P("section", "dp", "tensor"),
            P("section", None, "tensor"),
            P("section", None, None, ("dp", "tensor")),
            P("section", None, "tensor"),
            P("section", "tensor", "dp"),
            P("section", "dp", "tensor"),
            P("section", ("dp", "tensor"), None),
            P("section", "tensor", "dp"),
            P("section", None, "dp", "tensor"),
            P("section", "tensor", "dp"),
        ),
        check_vma=False,
    )
```

```python
import functools

import jax
import jax.numpy as jnp
import numpy as np
from jax import lax
from jax.experimental import pallas as pl
from jax.experimental.pallas import tpu as pltpu
from jax.sharding import PartitionSpec as P

HD = 64
NS = 128
AH = 8
KVH = 2
AD = 64
TAPS = 4
PAD = 128

EPS = 1e-06
ROPE_BASE = 100000000000.0
NEG = -1e30

F32 = jnp.float32
BF16 = jnp.bfloat16
HIGH = lax.Precision.HIGHEST
MIB = 1024 * 1024

CORE = [(i, i ^ 1) for i in range(4)]
FAR = [(i, i ^ 2) for i in range(4)]


def dot_nn(a, b, precision=None):
    return lax.dot_general(
        a, b, (((1,), (0,)), ((), ())), preferred_element_type=F32, precision=precision
    )


def dot_nt(a, b):
    return lax.dot_general(a, b, (((1,), (1,)), ((), ())), preferred_element_type=F32)


def dot_tn(a, b):
    return lax.dot_general(a, b, (((0,), (0,)), ((), ())), preferred_element_type=F32)


def sigmoid(a):
    return 1.0 / (1.0 + jnp.exp(-a))


def silu_slope(a, s):
    return s * (1.0 + a * (1.0 - s))


def assemble(core, dst, half, other):
    dst[core] = half[0]
    dst[2 + core] = half[1]
    dst[1 - core] = other[0]
    dst[3 - core] = other[1]


def rows_of(ref):
    blocks, rows, width = ref.shape
    return ref[...].reshape(blocks * rows, width)


def give_parts(core, full, scr, keep_ref, send_ref):
    scr[...] = full.astype(BF16).reshape(scr.shape)
    keep_ref[0] = scr[core]
    keep_ref[1] = scr[2 + core]
    send_ref[0] = scr[1 - core]
    send_ref[1] = scr[3 - core]


def lane_parity(rows, width=128):
    return lax.broadcasted_iota(jnp.int32, (rows, width), 1)


def partner(a):
    lane = lax.broadcasted_iota(jnp.int32, a.shape, 1)
    return jnp.where((lane & 32) == 0, pltpu.roll(a, 96, 1), pltpu.roll(a, 32, 1))


def shift_down(a, k):
    return a if k == 0 else pltpu.roll(a, k, 0)


def shift_up(a, k):
    return a if k == 0 else pltpu.roll(a, a.shape[0] - k, 0)


def mixer_front(xs, taps, wcat, table):
    length = xs.shape[0]
    inner = (wcat.shape[1] - 2 * NS - 256 - PAD) // 2
    chans = inner + 2 * NS
    cos_q, sin_q = table[0:length], table[length : 2 * length]
    seg = table[2 * length : 3 * length]
    seg_rows = jnp.transpose(seg)
    heads = table[3 * length : 3 * length + 8]
    r = lax.rsqrt(jnp.mean(xs * xs, axis=-1, keepdims=True) + EPS)
    normed = (xs * r * taps[5:6, :]).astype(BF16)
    proj = dot_nn(normed, wcat[...])
    z = proj[:, :inner]
    v = proj[:, inner : 2 * inner + 2 * NS]
    place = lax.broadcasted_iota(jnp.int32, (length, 1), 0)
    keeps = []
    for k in range(TAPS):
        earlier = shift_down(seg, k)
        same = (place >= k) & (earlier[:, 0:1] == seg[:, 0:1])
        keeps.append(jnp.where(same, 1.0, 0.0))
    pre = taps[0:1, :chans] * v
    for k in range(1, TAPS):
        pre = pre + taps[k : k + 1, :chans] * (shift_down(v, k) * keeps[k])
    psig = sigmoid(pre)
    conv = pre * psig
    xc = conv[:, :inner]
    b_low = conv[:, inner : inner + NS].astype(BF16)
    c_low = conv[:, inner + NS :].astype(BF16)
    gram = dot_nt(c_low, b_low)
    base = 2 * inner + 2 * NS
    q_raw = proj[:, base : base + 128]
    kv_raw = proj[:, base + 128 : base + 256]
    step_cols = proj[:, base + 256 :]
    raw = jnp.transpose(step_cols)[:8] + heads[:, 0:1]
    step = jnp.maximum(raw, 0.0) + jnp.log1p(jnp.exp(-jnp.abs(raw)))
    rate = jnp.exp(heads[:, 1:2])
    row = lax.broadcasted_iota(jnp.int32, (length, length), 0)
    col = lax.broadcasted_iota(jnp.int32, (length, length), 1)
    upper = jnp.where(row <= col, 1.0, 0.0)
    level = dot_nn(-rate * step, upper, HIGH)
    level_cols = jnp.transpose(
        jnp.concatenate([level, jnp.zeros((PAD - 8, length), F32)], axis=0)
    )
    allowed = (row >= col) & (seg[:, 0:1] == seg_rows[0:1, :])
    lane = lane_parity(length)
    low_half = lane < 64
    cos_kv = jnp.where(low_half, cos_q, 1.0)
    sin_kv = jnp.where(low_half, sin_q, 0.0)
    q_rot = q_raw * cos_q + partner(q_raw) * sin_q
    kv_rot = kv_raw * cos_kv + partner(kv_raw) * sin_kv
    q01 = q_rot.astype(BF16)
    q10 = pltpu.roll(q_rot, 64, 1).astype(BF16)
    kv = kv_rot.astype(BF16)
    vk = pltpu.roll(kv_rot, 64, 1).astype(BF16)
    zero = jnp.zeros((length, 128), BF16)

    def lo(a):
        return jnp.where(low_half, a, zero)

    def hi(a):
        return jnp.where(low_half, zero, a)

    return dict(
        normed=normed, z=z, v=v, keeps=keeps, pre=pre, psig=psig, xc=xc, b_low=b_low,
        c_low=c_low, gram=gram, raw=raw, step=step, rate=rate, level=level,
        level_cols=level_cols, allowed=allowed, q01=q01, q10=q10, kv=kv, vk=vk, lo=lo,
        hi=hi, inner=inner, length=length, row=row, col=col, rope=(cos_q, sin_q, cos_kv, sin_kv),
    )


def decay_of(f, h):
    diff = f["level_cols"][:, h : h + 1] - f["level"][h : h + 1, :]
    return jnp.exp(jnp.where(f["allowed"], diff, NEG))


def probs_of(f, h):
    lo, hi = f["lo"], f["hi"]
    qh = f["q01"] if h == 0 else f["q10"]
    scores = jnp.where(f["allowed"], dot_nt(lo(qh), f["kv"]) * (AD ** (-0.5)), NEG)
    peak = jnp.max(scores, axis=-1, keepdims=True)
    powers = jnp.exp(scores - peak)
    return powers / jnp.sum(powers, axis=-1, keepdims=True)


def mixer_fwd_kernel(
    t_ref, half, other, taps, wcat, wout, table, keep_ref, send_ref, x_scr, act, out_scr
):
    t = t_ref[0]
    assemble(t, x_scr, half, other)
    f = mixer_front(rows_of(x_scr).astype(F32), taps, wcat, table)
    lo, hi, inner = f["lo"], f["hi"], f["inner"]
    for p in range(inner // 128):
        cs = slice(128 * p, 128 * p + 128)
        xp = f["xc"][:, cs]
        xl = xp.astype(BF16)
        y = taps[4:5, cs] * xp
        for j, side in enumerate((lo, hi)):
            h = 2 * p + j
            w = f["gram"] * decay_of(f, h) * f["step"][h : h + 1, :]
            y = y + dot_nn(w.astype(BF16), side(xl))
        z = f["z"][:, cs]
        act[:, cs] = (y * (z * sigmoid(z))).astype(BF16)
    att = dot_nn(probs_of(f, 0).astype(BF16), lo(f["vk"]))
    att = att + dot_nn(probs_of(f, 1).astype(BF16), hi(f["kv"]))
    act[:, inner : inner + 128] = att.astype(BF16)
    give_parts(t, dot_nn(act[...], wout[...]), out_scr, keep_ref, send_ref)


def mixer_bwd_kernel(
    t_ref, half, other, g_half, g_other, taps, wcat, wout, table,
    keep_ref, send_ref, normed_ref, dy, act, dm_ref, small_ref, headg_ref,
    x_scr, dm_scr, out_scr,
):
    t = t_ref[0]
    assemble(t, x_scr, half, other)
    assemble(t, dm_scr, g_half, g_other)
    f = mixer_front(rows_of(x_scr).astype(F32), taps, wcat, table)
    lo, hi, inner, length = f["lo"], f["hi"], f["inner"], f["length"]
    normed_ref[...] = f["normed"]
    dm = rows_of(dm_scr)
    dm_ref[...] = dm
    dact = dot_nt(dm, wout[...])
    gram, step, rate = f["gram"], f["step"], f["rate"]
    lane = lax.broadcasted_iota(jnp.int32, (length, PAD), 1)
    sub = lax.broadcasted_iota(jnp.int32, (8, length), 0)
    d_gram = jnp.zeros((length, length), F32)
    row_sums = jnp.zeros((length, PAD), F32)
    d_step = jnp.zeros((8, length), F32)
    small_ref[...] = jnp.zeros_like(small_ref)
    d_parts = []
    for p in range(inner // 128):
        cs = slice(128 * p, 128 * p + 128)
        xp = f["xc"][:, cs]
        xl = xp.astype(BF16)
        z = f["z"][:, cs]
        zs = sigmoid(z)
        dg = dact[:, cs]
        ds_low = (dg * (z * zs)).astype(BF16)
        ds = ds_low.astype(F32)
        skip = taps[4:5, cs]
        y = skip * xp
        dxc = skip * ds
        for j, side in enumerate((lo, hi)):
            h = 2 * p + j
            e = decay_of(f, h)
            step_h = step[h : h + 1, :]
            w_low = (gram * e * step_h).astype(BF16)
            ds_h = side(ds_low)
            y = y + dot_nn(w_low, side(xl))
            dxc = dxc + dot_tn(w_low, ds_h)
            te = dot_nt(ds_h, xl) * e
            d_gram = d_gram + te * step_h
            tg = te * gram
            d_step = jnp.where(sub == h, jnp.sum(tg, axis=0, keepdims=True), d_step)
            row_sums = jnp.where(
                lane == h, jnp.sum(tg * step_h, axis=1, keepdims=True), row_sums
            )
        act[:, cs] = (y * (z * zs)).astype(BF16)
        dy[:, cs] = (dg * y * silu_slope(z, zs)).astype(BF16)
        small_ref[4:5, cs] = jnp.sum(ds * xp, axis=0, keepdims=True)
        d_parts.append(dxc)
    d_level = jnp.transpose(row_sums)[:8] - step * d_step
    later = jnp.where(f["row"] >= f["col"], 1.0, 0.0)
    tail = dot_nn(d_level, later, HIGH)
    d_step = d_step - rate * tail
    d_raw = d_step * sigmoid(f["raw"])
    d_decay = -rate * jnp.sum(step * tail, axis=1, keepdims=True)
    d_bias = jnp.sum(d_raw, axis=1, keepdims=True)
    lane8 = lax.broadcasted_iota(jnp.int32, (8, PAD), 1)
    headg_ref[...] = jnp.where(lane8 == 0, d_bias, jnp.where(lane8 == 1, d_decay, 0.0))
    base = 2 * inner + 2 * NS
    dy[:, base + 256 : base + 384] = jnp.transpose(
        jnp.concatenate([d_raw, jnp.zeros((PAD - 8, length), F32)], axis=0)
    ).astype(BF16)
    dg_low = d_gram.astype(BF16)
    d_parts.append(dot_tn(dg_low, f["c_low"]))
    d_parts.append(dot_nn(dg_low, f["b_low"]))
    for p, part in enumerate(d_parts):
        cs = slice(128 * p, 128 * p + 128)
        dp = part * silu_slope(f["pre"][:, cs], f["psig"][:, cs])
        v = f["v"][:, cs]
        dv = taps[0:1, cs] * dp
        small_ref[0:1, cs] = jnp.sum(dp * v, axis=0, keepdims=True)
        for k in range(1, TAPS):
            kept = dp * f["keeps"][k]
            dv = dv + taps[k : k + 1, cs] * shift_up(kept, k)
            small_ref[k : k + 1, cs] = jnp.sum(kept * shift_down(v, k), axis=0, keepdims=True)
        dy[:, inner + 128 * p : inner + 128 * p + 128] = dv.astype(BF16)
    da01f = dact[:, inner : inner + 128]
    da01 = da01f.astype(BF16)
    da10 = pltpu.roll(da01f, 64, 1).astype(BF16)
    p0 = probs_of(f, 0)
    p1 = probs_of(f, 1)
    p0l, p1l = p0.astype(BF16), p1.astype(BF16)
    att = dot_nn(p0l, lo(f["vk"])) + dot_nn(p1l, hi(f["kv"]))
    act[:, inner : inner + 128] = att.astype(BF16)
    d_value = dot_tn(p0l, hi(da10)) + dot_tn(p1l, hi(da01))
    dp0 = dot_nt(lo(da01), f["vk"])
    dp1 = dot_nt(hi(da01), f["kv"])
    ds0 = (p0 * (dp0 - jnp.sum(p0 * dp0, axis=-1, keepdims=True))).astype(BF16)
    ds1 = (p1 * (dp1 - jnp.sum(p1 * dp1, axis=-1, keepdims=True))).astype(BF16)
    scale = AD ** (-0.5)
    dq = (dot_nn(ds0, lo(f["kv"])) + dot_nn(ds1, hi(f["vk"]))) * scale
    dkv = (dot_tn(ds0, lo(f["q01"])) + dot_tn(ds1, lo(f["q10"]))) * scale + d_value
    cos_q, sin_q, cos_kv, sin_kv = f["rope"]
    dy[:, base : base + 128] = (dq * cos_q - partner(dq) * sin_q).astype(BF16)
    dy[:, base + 128 : base + 256] = (dkv * cos_kv - partner(dkv) * sin_kv).astype(BF16)
    give_parts(t, dot_nt(dy[...], wcat[...]), out_scr, keep_ref, send_ref)


def ffn_fwd_kernel(
    t_ref, half, other, wgu, wd, keep_ref, send_ref, n_scr, out_scr
):
    t = t_ref[0]
    assemble(t, n_scr, half, other)
    n2 = rows_of(n_scr)
    g = dot_nn(n2, wgu[0])
    u = dot_nn(n2, wgu[1])
    hidden = (g * sigmoid(g) * u).astype(BF16)
    give_parts(t, dot_nn(hidden, wd[...]), out_scr, keep_ref, send_ref)


def ffn_bwd_kernel(
    t_ref, half, other, g_half, g_other, wgu, wd,
    keep_ref, send_ref, n_ref, dgu, hid_ref, go_ref, n_scr, go_scr, out_scr,
):
    t = t_ref[0]
    assemble(t, n_scr, half, other)
    assemble(t, go_scr, g_half, g_other)
    n2 = rows_of(n_scr)
    go = rows_of(go_scr)
    n_ref[...] = n2
    go_ref[...] = go
    width = wd.shape[0]
    g = dot_nn(n2, wgu[0])
    u = dot_nn(n2, wgu[1])
    dh = dot_nt(go, wd[...])
    s = sigmoid(g)
    act = g * s
    hid_ref[...] = (act * u).astype(BF16)
    dg = (dh * u * silu_slope(g, s)).astype(BF16)
    du = (dh * act).astype(BF16)
    dgu[:, :width] = dg
    dgu[:, width:] = du
    give_parts(t, dot_nt(dg, wgu[0]) + dot_nt(du, wgu[1]), out_scr, keep_ref, send_ref)


def resid_norm_kernel(x, pair, far, gain, resid_ref, n_ref):
    a = x[...].astype(F32) + (pair[...].astype(F32) + far[...].astype(F32))
    resid_ref[...] = a
    r = lax.rsqrt(jnp.mean(a * a, axis=-1, keepdims=True) + EPS)
    n_ref[...] = (a * r * gain[...]).astype(BF16)


def norm_bwd_kernel(a_ref, pair, far, gain, base, d_ref, low_ref, dgain_ref):
    a = a_ref[...].astype(F32)
    dn = pair[...].astype(F32) + far[...].astype(F32)
    r = lax.rsqrt(jnp.mean(a * a, axis=-1, keepdims=True) + EPS)
    dgain_ref[...] = jnp.sum(dn * a * r, axis=(0, 1), keepdims=True)
    dng = dn * gain[...]
    inner = jnp.mean(dng * a, axis=-1, keepdims=True)
    d = base[...].astype(F32) + (r * dng - a * (r * r * r) * inner)
    d_ref[...] = d
    low_ref[...] = d.astype(BF16)


def wgrad_ffn_kernel(na, nb, ga, gb, dgua, dgub, ha, hb, out):
    width = dgua.shape[1]
    out[:, :width] = (dot_tn(na[...], dgua[...]) + dot_tn(nb[...], dgub[...])).astype(BF16)
    out[:, width:] = (dot_tn(ga[...], ha[...]) + dot_tn(gb[...], hb[...])).astype(BF16)


def wgrad_mix_kernel(inner, t_ref, na, nb, ga, gb, dya, dyb, aa, ab, out, keep, send, step, scr):
    t, kv_head = t_ref[0], t_ref[1]
    zu = 2 * inner
    bc = zu + 2 * NS
    full = dot_tn(na[...], dya[...]) + dot_tn(nb[...], dyb[...])
    out[:, :zu] = full[:, :zu].astype(BF16)
    out[:, zu : zu + 128] = full[:, bc : bc + 128].astype(BF16)
    step[...] = jnp.transpose(full[:, bc + 256 :])[:8]
    out[:, zu + 128 :] = (dot_tn(ga[...], aa[...]) + dot_tn(gb[...], ab[...])).astype(BF16)
    kv = full[:, bc + 128 : bc + 256]
    vk = pltpu.roll(kv, 64, 1)
    low_half = lane_parity(kv.shape[0]) < 64
    first = kv_head == 0
    k_pair = jnp.where(low_half == first, jnp.where(first, kv, vk), 0.0)
    v_pair = jnp.where(low_half == first, jnp.where(first, vk, kv), 0.0)
    shared = jnp.concatenate([full[:, zu:bc], k_pair, v_pair], axis=1).astype(BF16)
    groups, blocks, rows, cols = scr.shape
    scr[...] = shared.reshape(groups, blocks, rows, cols)
    for g in range(groups):
        at = slice(g * rows, (g + 1) * rows)
        keep[0, at] = scr[g, t]
        keep[1, at] = scr[g, 2 + t]
        send[0, at] = scr[g, 1 - t]
        send[1, at] = scr[g, 3 - t]


def pack_kernel(
    t_ref, mixer_in, state, query, mixer_out, output, keyval, step, wcat, wout, sems
):
    inner = mixer_in.shape[2]
    at = 2 * inner
    end = at + 2 * NS
    moves = [
        (mixer_in.at[0], wcat.at[:, pl.ds(0, inner)]),
        (mixer_in.at[1], wcat.at[:, pl.ds(inner, inner)]),
        (state.at[0], wcat.at[:, pl.ds(at, NS)]),
        (state.at[1], wcat.at[:, pl.ds(at + NS, NS)]),
        (query, wcat.at[:, pl.ds(end, 128)]),
        (mixer_out, wout.at[pl.ds(0, inner)]),
        (output, wout.at[pl.ds(inner, output.shape[0])]),
    ]
    copies = [pltpu.make_async_copy(a, b, sems.at[i]) for i, (a, b) in enumerate(moves)]
    for copy in copies:
        copy.start()
    keys = keyval[:, :128].astype(F32)
    values = keyval[:, 128:].astype(F32)
    low_half = lane_parity(keys.shape[0]) < 64
    first = t_ref[1] == 0
    keys = jnp.where(first, keys, pltpu.roll(keys, 64, 1))
    values = jnp.where(first, pltpu.roll(values, 64, 1), values)
    wcat[:, end + 128 : end + 256] = jnp.where(low_half, keys, values).astype(BF16)
    wcat[:, end + 256 :] = jnp.zeros((keys.shape[0], PAD), BF16)
    wcat[:, end + 256 : end + 256 + step.shape[1]] = step[...]
    for copy in copies:
        copy.wait()


def unpack_kernel(inner, packed, mixer_in, query, mixer_out, output):
    wide = packed[...].astype(F32)
    mixer_in[0] = wide[:, :inner]
    mixer_in[1] = wide[:, inner : 2 * inner]
    query[...] = wide[:, 2 * inner : 2 * inner + 128]
    outs = jnp.transpose(wide[:, 2 * inner + 128 :])
    mixer_out[...] = outs[:inner]
    output[...] = outs[inner:]


VM = pl.BlockSpec(memory_space=pltpu.VMEM)
SM = pl.BlockSpec(memory_space=pltpu.SMEM)


def sds(shape, dtype):
    return jax.ShapeDtypeStruct(tuple(shape), dtype)


def params(mib):
    return pltpu.CompilerParams(vmem_limit_bytes=mib * MIB)


def cost(flops, nbytes, trans=0):
    return pl.CostEstimate(flops=int(flops), bytes_accessed=int(nbytes), transcendentals=int(trans))


def mixer_fwd(t, pieces, w, table):
    _, rows, width = pieces[0].shape
    wcat, wout = w["wcat"], w["wout"]
    length = 4 * rows
    return pl.pallas_call(
        mixer_fwd_kernel,
        out_shape=[sds((2, rows, width), BF16)] * 2,
        in_specs=[SM] + [VM] * 6,
        out_specs=[VM] * 2,
        scratch_shapes=[
            pltpu.VMEM((4, rows, width), BF16),
            pltpu.VMEM((length, wout.shape[0]), BF16),
            pltpu.VMEM((4, rows, width), BF16),
        ],
        compiler_params=params(12),
        cost_estimate=cost(2 * length * (wcat.size + wout.size) * 2, 2 * (wcat.size + wout.size)),
        name="mixer_fwd",
    )(t, *pieces, w["taps"], wcat, wout, table)


def mixer_bwd(t, pieces, grads, w, table, inner):
    _, rows, width = pieces[0].shape
    wcat, wout = w["wcat"], w["wout"]
    length = 4 * rows
    return pl.pallas_call(
        mixer_bwd_kernel,
        out_shape=[
            sds((2, rows, width), BF16),
            sds((2, rows, width), BF16),
            sds((length, width), BF16),
            sds((length, wcat.shape[1]), BF16),
            sds((length, wout.shape[0]), BF16),
            sds((length, width), BF16),
            sds((8, inner + 2 * NS), F32),
            sds((8, PAD), F32),
        ],
        in_specs=[SM] + [VM] * 8,
        out_specs=[VM] * 8,
        scratch_shapes=[pltpu.VMEM((4, rows, width), BF16)] * 3,
        compiler_params=params(16),
        cost_estimate=cost(2 * length * (wcat.size + wout.size) * 5, 2 * (wcat.size + wout.size)),
        name="mixer_bwd",
    )(t, *pieces, *grads, w["taps"], wcat, wout, table)


def ffn_fwd(t, pieces, w):
    _, rows, width = pieces[0].shape
    wgu, wd = w["wgu"], w["wd"]
    return pl.pallas_call(
        ffn_fwd_kernel,
        out_shape=[sds((2, rows, width), BF16)] * 2,
        in_specs=[SM] + [VM] * 4,
        out_specs=[VM] * 2,
        scratch_shapes=[pltpu.VMEM((4, rows, width), BF16)] * 2,
        compiler_params=params(8),
        cost_estimate=cost(8 * rows * (wgu.size + wd.size), 2 * (wgu.size + wd.size)),
        name="ffn_fwd",
    )(t, *pieces, wgu, wd)


def ffn_bwd(t, pieces, grads, w):
    _, rows, width = pieces[0].shape
    wgu, wd = w["wgu"], w["wd"]
    length, units = 4 * rows, wd.shape[0]
    return pl.pallas_call(
        ffn_bwd_kernel,
        out_shape=[
            sds((2, rows, width), BF16),
            sds((2, rows, width), BF16),
            sds((length, width), BF16),
            sds((length, 2 * units), BF16),
            sds((length, units), BF16),
            sds((length, width), BF16),
        ],
        in_specs=[SM] + [VM] * 6,
        out_specs=[VM] * 6,
        scratch_shapes=[pltpu.VMEM((4, rows, width), BF16)] * 3,
        compiler_params=params(8),
        cost_estimate=cost(16 * rows * (wgu.size + wd.size), 2 * (wgu.size + wd.size)),
        name="ffn_bwd",
    )(t, *pieces, *grads, wgu, wd)


def whole_block(shape):
    return pl.BlockSpec(shape, lambda i: (0,) * len(shape))


def resid_norm(x, part, gain):
    return pl.pallas_call(
        resid_norm_kernel,
        out_shape=[sds(x.shape, F32), sds(x.shape, BF16)],
        in_specs=[VM] * 4,
        out_specs=[VM] * 2,
        compiler_params=params(4),
        cost_estimate=cost(10 * x.size, 12 * x.size),
        name="resid_norm",
    )(x, *part, gain)


def norm_bwd(a, part, gain, base):
    return pl.pallas_call(
        norm_bwd_kernel,
        out_shape=[sds(a.shape, F32), sds(a.shape, BF16), sds((1, 1, a.shape[2]), F32)],
        in_specs=[VM] * 5,
        out_specs=[VM] * 3,
        compiler_params=params(4),
        cost_estimate=cost(20 * a.size, 16 * a.size),
        name="norm_bwd",
    )(a, *part, gain, base)


def wgrad_ffn(saved):
    (na, ga, dgua, ha), (nb, gb, dgub, hb) = saved
    length, width = na.shape
    cols = dgua.shape[1] + ha.shape[1]
    block = pl.BlockSpec((length, 256), lambda i: (0, i))
    return pl.pallas_call(
        wgrad_ffn_kernel,
        grid=(width // 256,),
        out_shape=pltpu.HBM((width, cols), BF16),
        in_specs=[block] * 4 + [whole_block(dgua.shape)] * 2 + [whole_block(ha.shape)] * 2,
        out_specs=pl.BlockSpec((256, cols), lambda i: (i, 0)),
        compiler_params=params(8),
        cost_estimate=cost(4 * length * width * cols, 2 * width * cols),
        name="wgrad_ffn",
    )(na, nb, ga, gb, dgua, dgub, ha, hb)


def wgrad_mix(tk, saved, inner, rows16):
    (na, ga, dya, aa), (nb, gb, dyb, ab) = saved
    length, width = na.shape
    cols = 2 * inner + 128 + aa.shape[1]
    scols = 2 * NS + 256
    block = pl.BlockSpec((length, 256), lambda i: (0, i))
    part = pl.BlockSpec((2, 64, scols), lambda i: (0, i, 0))
    return pl.pallas_call(
        functools.partial(wgrad_mix_kernel, inner),
        grid=(width // 256,),
        out_shape=[pltpu.HBM((width, cols), BF16)] + [sds((2, width // 4, scols), BF16)] * 2
        + [sds((8, width), F32)],
        in_specs=[SM]
        + [block] * 4
        + [whole_block(dya.shape)] * 2
        + [whole_block(aa.shape)] * 2,
        out_specs=[pl.BlockSpec((256, cols), lambda i: (i, 0)), part, part]
        + [pl.BlockSpec((8, 256), lambda i: (0, i))],
        scratch_shapes=[pltpu.VMEM((64 // rows16, 4, rows16, scols), BF16)],
        compiler_params=params(14),
        cost_estimate=cost(4 * length * width * (cols + 384), 2 * width * (cols + 384)),
        name="wgrad_mix",
    )(tk, na, nb, ga, gb, dya, dyb, aa, ab)


def pack(tk, mixer_in, state, query, keyval, step, mixer_out, output):
    width = mixer_in.shape[1]
    cols = 2 * mixer_in.shape[2] + 2 * NS + 256 + PAD
    rows = mixer_out.shape[0] + output.shape[0]
    return pl.pallas_call(
        pack_kernel,
        out_shape=[sds((width, cols), BF16), sds((rows, width), BF16)],
        in_specs=[SM] + [pl.BlockSpec(memory_space=pl.ANY)] * 5 + [VM] * 2,
        out_specs=[VM] * 2,
        scratch_shapes=[pltpu.SemaphoreType.DMA((7,))],
        compiler_params=params(8),
        cost_estimate=cost(width * cols, 4 * width * cols),
        name="pack",
    )(tk, mixer_in, state, query, mixer_out, output, keyval, step)


def unpack(packed, inner):
    rows, cols = packed.shape
    heads = cols - 3 * inner - 128
    return pl.pallas_call(
        functools.partial(unpack_kernel, inner),
        out_shape=[
            sds((2, rows, inner), F32),
            sds((rows, 128), F32),
            sds((inner, rows), F32),
            sds((heads, rows), F32),
        ],
        in_specs=[VM],
        out_specs=[VM] * 4,
        compiler_params=params(8),
        cost_estimate=cost(rows * cols, 6 * rows * cols),
        name="unpack",
    )(packed)


def gather(half):
    return (half, lax.ppermute(half, "tensor", CORE))


def scatter(keep, send):
    recv = lax.ppermute(send, "tensor", CORE)
    pair = (keep.astype(F32) + recv.astype(F32)).astype(BF16)
    return (pair, lax.ppermute(pair, "tensor", FAR))


def in_turn(work, pieces):
    results = []
    for m, piece in enumerate(pieces):
        if results:
            pair = results[-1][0]
            pair, piece = lax.optimization_barrier((pair, piece))
        results.append(work(m, piece))
    return results


def rope_tables(length):
    half = AD // 2
    freq = np.float32(ROPE_BASE) ** (
        -(np.arange(half, dtype=np.float32) * np.float32(2.0) / np.float32(AD))
    )
    angles = np.arange(length, dtype=np.float32)[:, None] * freq[None, :].astype(np.float32)
    cos = np.cos(angles).astype(np.float32)
    sin = np.sin(angles).astype(np.float32)
    cos_h = np.concatenate([cos, cos], axis=1)
    sin_h = np.concatenate([-sin, sin], axis=1)
    return np.concatenate(
        [np.concatenate([cos_h, cos_h], axis=1), np.concatenate([sin_h, sin_h], axis=1)], axis=0
    )


def per_device(
    inputs,
    cotangent,
    segment_ids,
    norm_gains,
    mixer_in,
    state_proj,
    step_proj,
    conv_inner,
    conv_state,
    head_params,
    mixer_out,
    query_proj,
    keyval_proj,
    output_proj,
    gate_up,
    down_proj,
):
    section_now = lax.axis_index("section")
    tensor_now = lax.axis_index("tensor")
    dp_count = lax.axis_size("dp")
    tensor_count = lax.axis_size("tensor")
    micro_count = inputs.shape[0]
    width = inputs.shape[3]
    length = segment_ids.shape[2]
    inner = mixer_in.shape[3]
    heads_here = inner // HD
    units = down_proj.shape[1]
    micros = range(micro_count)

    gains = norm_gains[0].astype(F32)
    query_heads = query_proj.shape[2] // AD
    key_group = tensor_now * query_heads // (AH // KVH)
    core, far_at = tensor_now % 2, tensor_now // 2
    t = jnp.stack([core, key_group]).astype(jnp.int32)
    wcat, wout = pack(
        t,
        mixer_in[0],
        state_proj[0],
        query_proj[0],
        keyval_proj[0],
        step_proj[0],
        mixer_out[0],
        output_proj[0],
    )
    taps = jnp.concatenate([conv_inner[0], conv_state[0, 0], conv_state[0, 1]], axis=-1).astype(F32)
    chans = inner + 2 * NS
    taps = jnp.concatenate(
        [
            jnp.pad(taps, ((0, 0), (0, width - chans))),
            jnp.pad(jnp.repeat(head_params[0, 2], HD), (0, width - inner))[None],
            gains[0:1],
            jnp.zeros((2, width), F32),
        ],
        axis=0,
    )
    heads = jnp.pad(head_params[0].T, ((0, 8 - heads_here), (0, PAD - 3)))
    weights = dict(wcat=wcat, wout=wout, taps=taps, wgu=gate_up[0], wd=down_proj[0])
    gain1, gain2 = gains[0].reshape(1, 1, width), gains[1].reshape(1, 1, width)
    rope = jnp.asarray(rope_tables(length))
    tables = [
        jnp.concatenate(
            [
                rope,
                jnp.broadcast_to(segment_ids[m, 0].astype(F32)[:, None], (length, PAD)),
                heads,
            ],
            axis=0,
        )
        for m in micros
    ]

    def halves(own):
        far = lax.ppermute(own, "tensor", FAR)
        return jnp.where(far_at == 0, jnp.stack([own, far]), jnp.stack([far, own]))

    def own_of(half):
        return lax.dynamic_index_in_dim(half, far_at, 0, keepdims=False)

    def forward(x_own):
        pieces = [gather(x_own[m]) for m in micros]
        parts = in_turn(lambda m, p: scatter(*mixer_fwd(t, p, weights, tables[m])), pieces)
        resid, n2 = zip(*[resid_norm(x_own[m], parts[m], gain2) for m in micros])
        n_pieces = [gather(n2[m]) for m in micros]
        outs = in_turn(lambda m, p: scatter(*ffn_fwd(t, p, weights)), n_pieces)
        result = [
            (resid[m] + (outs[m][0].astype(F32) + outs[m][1].astype(F32))).astype(BF16)
            for m in micros
        ]
        return result, pieces, n_pieces, resid

    def backward(go, saved, x_own, last_pass):
        pieces, n_pieces, resid = saved
        g_pieces = [gather(go[m]) for m in micros]

        def ffn_part(m, grads):
            made = ffn_bwd(t, n_pieces[m], grads, weights)
            return scatter(*made[:2]) + (made,)

        ffn_all = in_turn(ffn_part, g_pieces)
        ffn = [got[2] for got in ffn_all]
        parts = [got[:2] for got in ffn_all]
        g_ffn = None
        if last_pass:
            g_ffn = wgrad_ffn([(ffn[m][2], ffn[m][5], ffn[m][3], ffn[m][4]) for m in micros])
            parts, g_ffn = lax.optimization_barrier((parts, g_ffn))
        mid = [norm_bwd(resid[m], parts[m], gain2, go[m]) for m in micros]
        d_pieces = [gather(mid[m][1]) for m in micros]

        def mix_part(m, grads):
            made = mixer_bwd(t, pieces[m], grads, weights, tables[m], inner)
            return scatter(*made[:2]) + (made,)

        mix_all = in_turn(mix_part, d_pieces)
        mix = [got[2] for got in mix_all]
        parts1 = [got[:2] for got in mix_all]
        low = [norm_bwd(x_own[m], parts1[m], gain1, mid[m][0]) for m in micros]
        return [low[m][1] for m in micros], g_ffn, mix, mid, low

    first = [halves(inputs[m, 0]) for m in micros]
    top = [halves(cotangent[m, 0]) for m in micros]

    out0, _, _, _ = forward(first)
    received = [lax.ppermute(out0[m], "section", [(0, 1)]) for m in micros]
    x_own = [jnp.where(section_now == 0, first[m], received[m]) for m in micros]
    out1, pieces, n_pieces, resid = forward(x_own)
    saved = (pieces, n_pieces, resid)
    grad1, _, _, _, _ = backward(top, saved, x_own, False)
    grad_in = [lax.ppermute(grad1[m], "section", [(1, 0)]) for m in micros]
    go = [jnp.where(section_now == 1, top[m], grad_in[m]) for m in micros]
    d_low, g_ffn, mix, mid, low = backward(go, saved, x_own, True)

    rows16 = width // (dp_count * tensor_count)
    r_ffn = lax.psum_scatter(g_ffn, "dp", scatter_dimension=0, tiled=True)
    g_mix, keep, send, g_step = wgrad_mix(
        t, [(mix[m][2], mix[m][5], mix[m][3], mix[m][4]) for m in micros], inner, rows16
    )
    recv = lax.ppermute(send, "tensor", CORE)
    pair = keep.astype(F32) + recv.astype(F32)
    last = lax.ppermute(
        lax.dynamic_index_in_dim(pair, 1 - far_at, 0, keepdims=False).astype(BF16), "tensor", FAR
    )
    shared = own_of(pair) + last.astype(F32)
    g_mix, r_ffn, shared, out1, d_low = lax.optimization_barrier(
        (g_mix, r_ffn, shared, out1, d_low)
    )
    r_mix = lax.psum_scatter(g_mix, "dp", scatter_dimension=0, tiled=True)
    step_to = dp_count // 2
    while step_to:
        shared = shared.reshape(2, shared.shape[0] // 2, shared.shape[1])
        side = lax.axis_index("dp") // step_to % 2
        give = lax.dynamic_index_in_dim(shared, 1 - side, 0, keepdims=False).astype(BF16)
        got = lax.ppermute(give, "dp", [(i, i ^ step_to) for i in range(dp_count)])
        shared = lax.dynamic_index_in_dim(shared, side, 0, keepdims=False) + got.astype(F32)
        step_to //= 2
    r_shared = shared

    small = sum(mix[m][6] for m in micros)
    headg = sum(mix[m][7] for m in micros)
    d_skip = small[4, :inner].reshape(heads_here, HD).sum(axis=1)
    over_all = jnp.concatenate(
        [
            sum(low[m][2] for m in micros)[0, 0] * 0.5,
            sum(mid[m][2] for m in micros)[0, 0] * 0.5,
            small[:TAPS, inner:].reshape(-1),
        ]
    )
    per_head = jnp.concatenate(
        [
            small[:TAPS, :inner].reshape(-1),
            headg[:heads_here, 0],
            headg[:heads_here, 1],
            d_skip,
            g_step[:heads_here].reshape(-1),
        ]
    )
    split_at = over_all.shape[0]
    vector = jnp.concatenate([over_all, per_head])
    bit = 1
    while bit < dp_count:
        vector = vector + lax.ppermute(vector, "dp", [(i, i ^ bit) for i in range(dp_count)])
        bit *= 2
    over_all, per_head = vector[:split_at], vector[split_at:]
    over_all = over_all + lax.ppermute(over_all, "tensor", CORE)
    over_all = over_all + lax.ppermute(over_all, "tensor", FAR)
    place = lax.axis_index("dp") * tensor_count + tensor_now
    pick = functools.partial(lax.dynamic_slice_in_dim, axis=1)
    grad_gains = pick(over_all[: 2 * width].reshape(2, width), place * rows16, rows16)
    state_taps = over_all[2 * width :].reshape(TAPS, 2, NS).transpose(1, 0, 2)
    each = NS // (dp_count * tensor_count)
    grad_conv_state = lax.dynamic_slice_in_dim(state_taps, place * each, each, axis=2)
    grad_conv_inner = per_head[: TAPS * inner].reshape(TAPS, inner)
    at = TAPS * inner + 3 * heads_here
    grad_heads = per_head[TAPS * inner : at].reshape(3, heads_here)
    step_rows = width // dp_count
    grad_step = lax.dynamic_slice_in_dim(
        per_head[at:].reshape(heads_here, width), lax.axis_index("dp") * step_rows, step_rows, axis=1
    ).T

    r_ffn = r_ffn.astype(F32)
    grad_gate_up = jnp.stack([r_ffn[:, :units], r_ffn[:, units : 2 * units]])
    grad_down = r_ffn[:, 2 * units :].T
    grad_mixer_in, grad_query, grad_mixer_out, grad_output = unpack(r_mix, inner)
    grad_state = jnp.stack([r_shared[:, :NS], r_shared[:, NS : 2 * NS]])
    grad_keyval = r_shared[:, 2 * NS :]
    return (
        jnp.stack([own_of(h) for h in out1])[None, :, None],
        jnp.stack([own_of(h) for h in d_low])[None, :, None],
        grad_gains[None],
        grad_mixer_in[None],
        grad_state[None],
        grad_step[None],
        grad_conv_inner[None],
        grad_conv_state[None],
        grad_heads[None],
        grad_mixer_out[None],
        grad_query[None],
        grad_keyval[None],
        grad_output[None],
        grad_gate_up[None],
        grad_down[None],
    )


def solution(mesh):
    placed = (
        P(None, "dp", "tensor", None),
        P(None, "dp", "tensor", None),
        P(None, "dp", None),
        P("section", None, None),
        P("section", None, None, "tensor"),
        P("section", None, None, None),
        P("section", None, "tensor"),
        P("section", None, "tensor"),
        P("section", None, None, None),
        P("section", None, "tensor"),
        P("section", "tensor", None),
        P("section", None, "tensor"),
        P("section", None, None),
        P("section", "tensor", None),
        P("section", None, None, "tensor"),
        P("section", "tensor", None),
    )
    return jax.shard_map(
        per_device,
        mesh=mesh,
        in_specs=placed,
        out_specs=(
            P("section", None, "dp", "tensor", None),
            P("section", None, "dp", "tensor", None),
            P("section", None, ("dp", "tensor")),
            P("section", None, "dp", "tensor"),
            P("section", None, ("dp", "tensor"), None),
            P("section", "dp", "tensor"),
            P("section", None, "tensor"),
            P("section", None, None, ("dp", "tensor")),
            P("section", None, "tensor"),
            P("section", "tensor", "dp"),
            P("section", "dp", "tensor"),
            P("section", ("dp", "tensor"), None),
            P("section", "tensor", "dp"),
            P("section", None, "dp", "tensor"),
            P("section", "tensor", "dp"),
        ),
        check_vma=False,
    )
```

```python
import functools

import jax
import jax.numpy as jnp
import numpy as np
from jax import lax
from jax.experimental import pallas as pl
from jax.experimental.pallas import tpu as pltpu
from jax.sharding import PartitionSpec as P

HD = 64
NS = 128
AH = 8
KVH = 2
AD = 64
TAPS = 4
PAD = 128

EPS = 1e-06
ROPE_BASE = 100000000000.0
NEG = -1e30

F32 = jnp.float32
BF16 = jnp.bfloat16
HIGH = lax.Precision.HIGHEST
MIB = 1024 * 1024

CORE = [(i, i ^ 1) for i in range(4)]
FAR = [(i, i ^ 2) for i in range(4)]


def dot_nn(a, b, precision=None):
    return lax.dot_general(
        a, b, (((1,), (0,)), ((), ())), preferred_element_type=F32, precision=precision
    )


def dot_nt(a, b):
    return lax.dot_general(a, b, (((1,), (1,)), ((), ())), preferred_element_type=F32)


def dot_tn(a, b):
    return lax.dot_general(a, b, (((0,), (0,)), ((), ())), preferred_element_type=F32)


def sigmoid(a):
    return 1.0 / (1.0 + jnp.exp(-a))


def silu_slope(a, s):
    return s * (1.0 + a * (1.0 - s))


def assemble(core, dst, half, other):
    dst[core] = half[0]
    dst[2 + core] = half[1]
    dst[1 - core] = other[0]
    dst[3 - core] = other[1]


def rows_of(ref):
    blocks, rows, width = ref.shape
    return ref[...].reshape(blocks * rows, width)


def give_parts(core, full, scr, keep_ref, send_ref):
    scr[...] = full.astype(BF16).reshape(scr.shape)
    keep_ref[0] = scr[core]
    keep_ref[1] = scr[2 + core]
    send_ref[0] = scr[1 - core]
    send_ref[1] = scr[3 - core]


def lane_parity(rows, width=128):
    return lax.broadcasted_iota(jnp.int32, (rows, width), 1)


def partner(a):
    lane = lax.broadcasted_iota(jnp.int32, a.shape, 1)
    return jnp.where((lane & 32) == 0, pltpu.roll(a, 96, 1), pltpu.roll(a, 32, 1))


def shift_down(a, k):
    return a if k == 0 else pltpu.roll(a, k, 0)


def shift_up(a, k):
    return a if k == 0 else pltpu.roll(a, a.shape[0] - k, 0)


def mixer_front(xs, taps, wcat, table):
    length = xs.shape[0]
    inner = (wcat.shape[1] - 2 * NS - 256 - PAD) // 2
    chans = inner + 2 * NS
    cos_q, sin_q = table[0:length], table[length : 2 * length]
    seg = table[2 * length : 3 * length]
    seg_rows = jnp.transpose(seg)
    heads = table[3 * length : 3 * length + 8]
    r = lax.rsqrt(jnp.mean(xs * xs, axis=-1, keepdims=True) + EPS)
    normed = (xs * r * taps[5:6, :]).astype(BF16)
    proj = dot_nn(normed, wcat[...])
    z = proj[:, :inner]
    v = proj[:, inner : 2 * inner + 2 * NS]
    place = lax.broadcasted_iota(jnp.int32, (length, 1), 0)
    keeps = []
    for k in range(TAPS):
        earlier = shift_down(seg, k)
        same = (place >= k) & (earlier[:, 0:1] == seg[:, 0:1])
        keeps.append(jnp.where(same, 1.0, 0.0))
    pre = taps[0:1, :chans] * v
    for k in range(1, TAPS):
        pre = pre + taps[k : k + 1, :chans] * (shift_down(v, k) * keeps[k])
    psig = sigmoid(pre)
    conv = pre * psig
    xc = conv[:, :inner]
    b_low = conv[:, inner : inner + NS].astype(BF16)
    c_low = conv[:, inner + NS :].astype(BF16)
    gram = dot_nt(c_low, b_low)
    base = 2 * inner + 2 * NS
    q_raw = proj[:, base : base + 128]
    kv_raw = proj[:, base + 128 : base + 256]
    step_cols = proj[:, base + 256 :]
    raw = jnp.transpose(step_cols)[:8] + heads[:, 0:1]
    step = jnp.maximum(raw, 0.0) + jnp.log1p(jnp.exp(-jnp.abs(raw)))
    rate = jnp.exp(heads[:, 1:2])
    row = lax.broadcasted_iota(jnp.int32, (length, length), 0)
    col = lax.broadcasted_iota(jnp.int32, (length, length), 1)
    upper = jnp.where(row <= col, 1.0, 0.0)
    level = dot_nn(-rate * step, upper, HIGH)
    level_cols = jnp.transpose(
        jnp.concatenate([level, jnp.zeros((PAD - 8, length), F32)], axis=0)
    )
    allowed = (row >= col) & (seg[:, 0:1] == seg_rows[0:1, :])
    lane = lane_parity(length)
    low_half = lane < 64
    cos_kv = jnp.where(low_half, cos_q, 1.0)
    sin_kv = jnp.where(low_half, sin_q, 0.0)
    q_rot = q_raw * cos_q + partner(q_raw) * sin_q
    kv_rot = kv_raw * cos_kv + partner(kv_raw) * sin_kv
    q01 = q_rot.astype(BF16)
    q10 = pltpu.roll(q_rot, 64, 1).astype(BF16)
    kv = kv_rot.astype(BF16)
    vk = pltpu.roll(kv_rot, 64, 1).astype(BF16)
    zero = jnp.zeros((length, 128), BF16)

    def lo(a):
        return jnp.where(low_half, a, zero)

    def hi(a):
        return jnp.where(low_half, zero, a)

    return dict(
        normed=normed, z=z, v=v, keeps=keeps, pre=pre, psig=psig, xc=xc, b_low=b_low,
        c_low=c_low, gram=gram, raw=raw, step=step, rate=rate, level=level,
        level_cols=level_cols, allowed=allowed, q01=q01, q10=q10, kv=kv, vk=vk, lo=lo,
        hi=hi, inner=inner, length=length, row=row, col=col, rope=(cos_q, sin_q, cos_kv, sin_kv),
    )


def decay_of(f, h):
    diff = f["level_cols"][:, h : h + 1] - f["level"][h : h + 1, :]
    return jnp.exp(jnp.where(f["allowed"], diff, NEG))


def probs_of(f, h):
    lo, hi = f["lo"], f["hi"]
    qh = f["q01"] if h == 0 else f["q10"]
    scores = jnp.where(f["allowed"], dot_nt(lo(qh), f["kv"]) * (AD ** (-0.5)), NEG)
    peak = jnp.max(scores, axis=-1, keepdims=True)
    powers = jnp.exp(scores - peak)
    return powers / jnp.sum(powers, axis=-1, keepdims=True)


def mixer_fwd_kernel(
    t_ref, half, other, taps, wcat, wout, table, keep_ref, send_ref, x_scr, act, out_scr
):
    t = t_ref[0]
    assemble(t, x_scr, half, other)
    f = mixer_front(rows_of(x_scr).astype(F32), taps, wcat, table)
    lo, hi, inner = f["lo"], f["hi"], f["inner"]
    for p in range(inner // 128):
        cs = slice(128 * p, 128 * p + 128)
        xp = f["xc"][:, cs]
        xl = xp.astype(BF16)
        y = taps[4:5, cs] * xp
        for j, side in enumerate((lo, hi)):
            h = 2 * p + j
            w = f["gram"] * decay_of(f, h) * f["step"][h : h + 1, :]
            y = y + dot_nn(w.astype(BF16), side(xl))
        z = f["z"][:, cs]
        act[:, cs] = (y * (z * sigmoid(z))).astype(BF16)
    att = dot_nn(probs_of(f, 0).astype(BF16), lo(f["vk"]))
    att = att + dot_nn(probs_of(f, 1).astype(BF16), hi(f["kv"]))
    act[:, inner : inner + 128] = att.astype(BF16)
    give_parts(t, dot_nn(act[...], wout[...]), out_scr, keep_ref, send_ref)


def mixer_bwd_kernel(
    t_ref, half, other, g_half, g_other, taps, wcat, wout, table,
    keep_ref, send_ref, normed_ref, dy, act, dm_ref, small_ref, headg_ref,
    x_scr, dm_scr, out_scr,
):
    t = t_ref[0]
    assemble(t, x_scr, half, other)
    assemble(t, dm_scr, g_half, g_other)
    f = mixer_front(rows_of(x_scr).astype(F32), taps, wcat, table)
    lo, hi, inner, length = f["lo"], f["hi"], f["inner"], f["length"]
    normed_ref[...] = f["normed"]
    dm = rows_of(dm_scr)
    dm_ref[...] = dm
    dact = dot_nt(dm, wout[...])
    gram, step, rate = f["gram"], f["step"], f["rate"]
    lane = lax.broadcasted_iota(jnp.int32, (length, PAD), 1)
    sub = lax.broadcasted_iota(jnp.int32, (8, length), 0)
    d_gram = jnp.zeros((length, length), F32)
    row_sums = jnp.zeros((length, PAD), F32)
    d_step = jnp.zeros((8, length), F32)
    small_ref[...] = jnp.zeros_like(small_ref)
    d_parts = []
    for p in range(inner // 128):
        cs = slice(128 * p, 128 * p + 128)
        xp = f["xc"][:, cs]
        xl = xp.astype(BF16)
        z = f["z"][:, cs]
        zs = sigmoid(z)
        dg = dact[:, cs]
        ds_low = (dg * (z * zs)).astype(BF16)
        ds = ds_low.astype(F32)
        skip = taps[4:5, cs]
        y = skip * xp
        dxc = skip * ds
        for j, side in enumerate((lo, hi)):
            h = 2 * p + j
            e = decay_of(f, h)
            step_h = step[h : h + 1, :]
            w_low = (gram * e * step_h).astype(BF16)
            ds_h = side(ds_low)
            y = y + dot_nn(w_low, side(xl))
            dxc = dxc + dot_tn(w_low, ds_h)
            te = dot_nt(ds_h, xl) * e
            d_gram = d_gram + te * step_h
            tg = te * gram
            d_step = jnp.where(sub == h, jnp.sum(tg, axis=0, keepdims=True), d_step)
            row_sums = jnp.where(
                lane == h, jnp.sum(tg * step_h, axis=1, keepdims=True), row_sums
            )
        act[:, cs] = (y * (z * zs)).astype(BF16)
        dy[:, cs] = (dg * y * silu_slope(z, zs)).astype(BF16)
        small_ref[4:5, cs] = jnp.sum(ds * xp, axis=0, keepdims=True)
        d_parts.append(dxc)
    d_level = jnp.transpose(row_sums)[:8] - step * d_step
    later = jnp.where(f["row"] >= f["col"], 1.0, 0.0)
    tail = dot_nn(d_level, later, HIGH)
    d_step = d_step - rate * tail
    d_raw = d_step * sigmoid(f["raw"])
    d_decay = -rate * jnp.sum(step * tail, axis=1, keepdims=True)
    d_bias = jnp.sum(d_raw, axis=1, keepdims=True)
    lane8 = lax.broadcasted_iota(jnp.int32, (8, PAD), 1)
    headg_ref[...] = jnp.where(lane8 == 0, d_bias, jnp.where(lane8 == 1, d_decay, 0.0))
    base = 2 * inner + 2 * NS
    dy[:, base + 256 : base + 384] = jnp.transpose(
        jnp.concatenate([d_raw, jnp.zeros((PAD - 8, length), F32)], axis=0)
    ).astype(BF16)
    dg_low = d_gram.astype(BF16)
    d_parts.append(dot_tn(dg_low, f["c_low"]))
    d_parts.append(dot_nn(dg_low, f["b_low"]))
    for p, part in enumerate(d_parts):
        cs = slice(128 * p, 128 * p + 128)
        dp = part * silu_slope(f["pre"][:, cs], f["psig"][:, cs])
        v = f["v"][:, cs]
        dv = taps[0:1, cs] * dp
        small_ref[0:1, cs] = jnp.sum(dp * v, axis=0, keepdims=True)
        for k in range(1, TAPS):
            kept = dp * f["keeps"][k]
            dv = dv + taps[k : k + 1, cs] * shift_up(kept, k)
            small_ref[k : k + 1, cs] = jnp.sum(kept * shift_down(v, k), axis=0, keepdims=True)
        dy[:, inner + 128 * p : inner + 128 * p + 128] = dv.astype(BF16)
    da01f = dact[:, inner : inner + 128]
    da01 = da01f.astype(BF16)
    da10 = pltpu.roll(da01f, 64, 1).astype(BF16)
    p0 = probs_of(f, 0)
    p1 = probs_of(f, 1)
    p0l, p1l = p0.astype(BF16), p1.astype(BF16)
    att = dot_nn(p0l, lo(f["vk"])) + dot_nn(p1l, hi(f["kv"]))
    act[:, inner : inner + 128] = att.astype(BF16)
    d_value = dot_tn(p0l, hi(da10)) + dot_tn(p1l, hi(da01))
    dp0 = dot_nt(lo(da01), f["vk"])
    dp1 = dot_nt(hi(da01), f["kv"])
    ds0 = (p0 * (dp0 - jnp.sum(p0 * dp0, axis=-1, keepdims=True))).astype(BF16)
    ds1 = (p1 * (dp1 - jnp.sum(p1 * dp1, axis=-1, keepdims=True))).astype(BF16)
    scale = AD ** (-0.5)
    dq = (dot_nn(ds0, lo(f["kv"])) + dot_nn(ds1, hi(f["vk"]))) * scale
    dkv = (dot_tn(ds0, lo(f["q01"])) + dot_tn(ds1, lo(f["q10"]))) * scale + d_value
    cos_q, sin_q, cos_kv, sin_kv = f["rope"]
    dy[:, base : base + 128] = (dq * cos_q - partner(dq) * sin_q).astype(BF16)
    dy[:, base + 128 : base + 256] = (dkv * cos_kv - partner(dkv) * sin_kv).astype(BF16)
    give_parts(t, dot_nt(dy[...], wcat[...]), out_scr, keep_ref, send_ref)


def ffn_fwd_kernel(
    t_ref, half, other, wgu, wd, keep_ref, send_ref, n_scr, out_scr
):
    t = t_ref[0]
    assemble(t, n_scr, half, other)
    n2 = rows_of(n_scr)
    g = dot_nn(n2, wgu[0])
    u = dot_nn(n2, wgu[1])
    hidden = (g * sigmoid(g) * u).astype(BF16)
    give_parts(t, dot_nn(hidden, wd[...]), out_scr, keep_ref, send_ref)


def ffn_bwd_kernel(
    t_ref, half, other, g_half, g_other, wgu, wd,
    keep_ref, send_ref, n_ref, dgu, hid_ref, go_ref, n_scr, go_scr, out_scr,
):
    t = t_ref[0]
    assemble(t, n_scr, half, other)
    assemble(t, go_scr, g_half, g_other)
    n2 = rows_of(n_scr)
    go = rows_of(go_scr)
    n_ref[...] = n2
    go_ref[...] = go
    width = wd.shape[0]
    g = dot_nn(n2, wgu[0])
    u = dot_nn(n2, wgu[1])
    dh = dot_nt(go, wd[...])
    s = sigmoid(g)
    act = g * s
    hid_ref[...] = (act * u).astype(BF16)
    dg = (dh * u * silu_slope(g, s)).astype(BF16)
    du = (dh * act).astype(BF16)
    dgu[:, :width] = dg
    dgu[:, width:] = du
    give_parts(t, dot_nt(dg, wgu[0]) + dot_nt(du, wgu[1]), out_scr, keep_ref, send_ref)


def resid_norm_kernel(x, pair, far, gain, resid_ref, n_ref):
    a = x[...].astype(F32) + (pair[...].astype(F32) + far[...].astype(F32))
    resid_ref[...] = a
    r = lax.rsqrt(jnp.mean(a * a, axis=-1, keepdims=True) + EPS)
    n_ref[...] = (a * r * gain[...]).astype(BF16)


def norm_bwd_kernel(a_ref, pair, far, gain, base, d_ref, low_ref, dgain_ref):
    a = a_ref[...].astype(F32)
    dn = pair[...].astype(F32) + far[...].astype(F32)
    r = lax.rsqrt(jnp.mean(a * a, axis=-1, keepdims=True) + EPS)
    dgain_ref[...] = jnp.sum(dn * a * r, axis=(0, 1), keepdims=True)
    dng = dn * gain[...]
    inner = jnp.mean(dng * a, axis=-1, keepdims=True)
    d = base[...].astype(F32) + (r * dng - a * (r * r * r) * inner)
    d_ref[...] = d
    low_ref[...] = d.astype(BF16)


def wgrad_ffn_kernel(na, nb, ga, gb, dgua, dgub, ha, hb, out):
    width = dgua.shape[1]
    out[:, :width] = (dot_tn(na[...], dgua[...]) + dot_tn(nb[...], dgub[...])).astype(BF16)
    out[:, width:] = (dot_tn(ga[...], ha[...]) + dot_tn(gb[...], hb[...])).astype(BF16)


def wgrad_mix_kernel(inner, t_ref, na, nb, ga, gb, dya, dyb, aa, ab, out, keep, send, step, scr):
    t, kv_head = t_ref[0], t_ref[1]
    zu = 2 * inner
    bc = zu + 2 * NS
    full = dot_tn(na[...], dya[...]) + dot_tn(nb[...], dyb[...])
    out[:, :zu] = full[:, :zu].astype(BF16)
    out[:, zu : zu + 128] = full[:, bc : bc + 128].astype(BF16)
    step[...] = jnp.transpose(full[:, bc + 256 :])[:8]
    out[:, zu + 128 :] = (dot_tn(ga[...], aa[...]) + dot_tn(gb[...], ab[...])).astype(BF16)
    kv = full[:, bc + 128 : bc + 256]
    vk = pltpu.roll(kv, 64, 1)
    low_half = lane_parity(kv.shape[0]) < 64
    first = kv_head == 0
    k_pair = jnp.where(low_half == first, jnp.where(first, kv, vk), 0.0)
    v_pair = jnp.where(low_half == first, jnp.where(first, vk, kv), 0.0)
    shared = jnp.concatenate([full[:, zu:bc], k_pair, v_pair], axis=1).astype(BF16)
    groups, blocks, rows, cols = scr.shape
    scr[...] = shared.reshape(groups, blocks, rows, cols)
    for g in range(groups):
        at = slice(g * rows, (g + 1) * rows)
        keep[0, at] = scr[g, t]
        keep[1, at] = scr[g, 2 + t]
        send[0, at] = scr[g, 1 - t]
        send[1, at] = scr[g, 3 - t]


def pack_kernel(
    t_ref, mixer_in, state, query, mixer_out, output, keyval, step, wcat, wout, sems
):
    inner = mixer_in.shape[2]
    at = 2 * inner
    end = at + 2 * NS
    moves = [
        (mixer_in.at[0], wcat.at[:, pl.ds(0, inner)]),
        (mixer_in.at[1], wcat.at[:, pl.ds(inner, inner)]),
        (state.at[0], wcat.at[:, pl.ds(at, NS)]),
        (state.at[1], wcat.at[:, pl.ds(at + NS, NS)]),
        (query, wcat.at[:, pl.ds(end, 128)]),
        (mixer_out, wout.at[pl.ds(0, inner)]),
        (output, wout.at[pl.ds(inner, output.shape[0])]),
    ]
    copies = [pltpu.make_async_copy(a, b, sems.at[i]) for i, (a, b) in enumerate(moves)]
    for copy in copies:
        copy.start()
    keys = keyval[:, :128].astype(F32)
    values = keyval[:, 128:].astype(F32)
    low_half = lane_parity(keys.shape[0]) < 64
    first = t_ref[1] == 0
    keys = jnp.where(first, keys, pltpu.roll(keys, 64, 1))
    values = jnp.where(first, pltpu.roll(values, 64, 1), values)
    wcat[:, end + 128 : end + 256] = jnp.where(low_half, keys, values).astype(BF16)
    wcat[:, end + 256 :] = jnp.zeros((keys.shape[0], PAD), BF16)
    wcat[:, end + 256 : end + 256 + step.shape[1]] = step[...]
    for copy in copies:
        copy.wait()


def unpack_kernel(inner, packed, mixer_in, query, mixer_out, output):
    wide = packed[...].astype(F32)
    mixer_in[0] = wide[:, :inner]
    mixer_in[1] = wide[:, inner : 2 * inner]
    query[...] = wide[:, 2 * inner : 2 * inner + 128]
    outs = jnp.transpose(wide[:, 2 * inner + 128 :])
    mixer_out[...] = outs[:inner]
    output[...] = outs[inner:]


VM = pl.BlockSpec(memory_space=pltpu.VMEM)
SM = pl.BlockSpec(memory_space=pltpu.SMEM)


def sds(shape, dtype):
    return jax.ShapeDtypeStruct(tuple(shape), dtype)


def params(mib):
    return pltpu.CompilerParams(vmem_limit_bytes=mib * MIB)


def cost(flops, nbytes, trans=0):
    return pl.CostEstimate(flops=int(flops), bytes_accessed=int(nbytes), transcendentals=int(trans))


def mixer_fwd(t, pieces, w, table):
    _, rows, width = pieces[0].shape
    wcat, wout = w["wcat"], w["wout"]
    length = 4 * rows
    return pl.pallas_call(
        mixer_fwd_kernel,
        out_shape=[sds((2, rows, width), BF16)] * 2,
        in_specs=[SM] + [VM] * 6,
        out_specs=[VM] * 2,
        scratch_shapes=[
            pltpu.VMEM((4, rows, width), BF16),
            pltpu.VMEM((length, wout.shape[0]), BF16),
            pltpu.VMEM((4, rows, width), BF16),
        ],
        compiler_params=params(12),
        cost_estimate=cost(2 * length * (wcat.size + wout.size) * 2, 2 * (wcat.size + wout.size)),
        name="mixer_fwd",
    )(t, *pieces, w["taps"], wcat, wout, table)


def mixer_bwd(t, pieces, grads, w, table, inner, last_pass):
    _, rows, width = pieces[0].shape
    wcat, wout = w["wcat"], w["wout"]
    length = 4 * rows
    kept = [
        ((length, width), BF16),
        ((length, wcat.shape[1]), BF16),
        ((length, wout.shape[0]), BF16),
        ((length, width), BF16),
        ((8, inner + 2 * NS), F32),
        ((8, PAD), F32),
    ]
    sent = [sds((2, rows, width), BF16)] * 2
    blocks = [pltpu.VMEM((4, rows, width), BF16)] * 3
    return pl.pallas_call(
        mixer_bwd_kernel,
        out_shape=sent + ([sds(*k) for k in kept] if last_pass else []),
        in_specs=[SM] + [VM] * 8,
        out_specs=[VM] * (8 if last_pass else 2),
        scratch_shapes=([] if last_pass else [pltpu.VMEM(*k) for k in kept]) + blocks,
        compiler_params=params(16),
        cost_estimate=cost(2 * length * (wcat.size + wout.size) * 5, 2 * (wcat.size + wout.size)),
        name="mixer_bwd",
    )(t, *pieces, *grads, w["taps"], wcat, wout, table)


def ffn_fwd(t, pieces, w):
    _, rows, width = pieces[0].shape
    wgu, wd = w["wgu"], w["wd"]
    return pl.pallas_call(
        ffn_fwd_kernel,
        out_shape=[sds((2, rows, width), BF16)] * 2,
        in_specs=[SM] + [VM] * 4,
        out_specs=[VM] * 2,
        scratch_shapes=[pltpu.VMEM((4, rows, width), BF16)] * 2,
        compiler_params=params(8),
        cost_estimate=cost(8 * rows * (wgu.size + wd.size), 2 * (wgu.size + wd.size)),
        name="ffn_fwd",
    )(t, *pieces, wgu, wd)


def ffn_bwd(t, pieces, grads, w, last_pass):
    _, rows, width = pieces[0].shape
    wgu, wd = w["wgu"], w["wd"]
    length, units = 4 * rows, wd.shape[0]
    kept = [
        ((length, width), BF16),
        ((length, 2 * units), BF16),
        ((length, units), BF16),
        ((length, width), BF16),
    ]
    sent = [sds((2, rows, width), BF16)] * 2
    blocks = [pltpu.VMEM((4, rows, width), BF16)] * 3
    return pl.pallas_call(
        ffn_bwd_kernel,
        out_shape=sent + ([sds(*k) for k in kept] if last_pass else []),
        in_specs=[SM] + [VM] * 6,
        out_specs=[VM] * (6 if last_pass else 2),
        scratch_shapes=([] if last_pass else [pltpu.VMEM(*k) for k in kept]) + blocks,
        compiler_params=params(10),
        cost_estimate=cost(16 * rows * (wgu.size + wd.size), 2 * (wgu.size + wd.size)),
        name="ffn_bwd",
    )(t, *pieces, *grads, wgu, wd)


def whole_block(shape):
    return pl.BlockSpec(shape, lambda i: (0,) * len(shape))


def resid_norm(x, part, gain):
    return pl.pallas_call(
        resid_norm_kernel,
        out_shape=[sds(x.shape, F32), sds(x.shape, BF16)],
        in_specs=[VM] * 4,
        out_specs=[VM] * 2,
        compiler_params=params(4),
        cost_estimate=cost(10 * x.size, 12 * x.size),
        name="resid_norm",
    )(x, *part, gain)


def norm_bwd(a, part, gain, base):
    return pl.pallas_call(
        norm_bwd_kernel,
        out_shape=[sds(a.shape, F32), sds(a.shape, BF16), sds((1, 1, a.shape[2]), F32)],
        in_specs=[VM] * 5,
        out_specs=[VM] * 3,
        compiler_params=params(4),
        cost_estimate=cost(20 * a.size, 16 * a.size),
        name="norm_bwd",
    )(a, *part, gain, base)


def wgrad_ffn(saved):
    (na, ga, dgua, ha), (nb, gb, dgub, hb) = saved
    length, width = na.shape
    cols = dgua.shape[1] + ha.shape[1]
    block = pl.BlockSpec((length, 256), lambda i: (0, i))
    return pl.pallas_call(
        wgrad_ffn_kernel,
        grid=(width // 256,),
        out_shape=pltpu.HBM((width, cols), BF16),
        in_specs=[block] * 4 + [whole_block(dgua.shape)] * 2 + [whole_block(ha.shape)] * 2,
        out_specs=pl.BlockSpec((256, cols), lambda i: (i, 0)),
        compiler_params=params(8),
        cost_estimate=cost(4 * length * width * cols, 2 * width * cols),
        name="wgrad_ffn",
    )(na, nb, ga, gb, dgua, dgub, ha, hb)


def wgrad_mix(tk, saved, inner, rows16):
    (na, ga, dya, aa), (nb, gb, dyb, ab) = saved
    length, width = na.shape
    cols = 2 * inner + 128 + aa.shape[1]
    scols = 2 * NS + 256
    block = pl.BlockSpec((length, 256), lambda i: (0, i))
    part = pl.BlockSpec((2, 64, scols), lambda i: (0, i, 0))
    return pl.pallas_call(
        functools.partial(wgrad_mix_kernel, inner),
        grid=(width // 256,),
        out_shape=[pltpu.HBM((width, cols), BF16)] + [sds((2, width // 4, scols), BF16)] * 2
        + [sds((8, width), F32)],
        in_specs=[SM]
        + [block] * 4
        + [whole_block(dya.shape)] * 2
        + [whole_block(aa.shape)] * 2,
        out_specs=[pl.BlockSpec((256, cols), lambda i: (i, 0)), part, part]
        + [pl.BlockSpec((8, 256), lambda i: (0, i))],
        scratch_shapes=[pltpu.VMEM((64 // rows16, 4, rows16, scols), BF16)],
        compiler_params=params(14),
        cost_estimate=cost(4 * length * width * (cols + 384), 2 * width * (cols + 384)),
        name="wgrad_mix",
    )(tk, na, nb, ga, gb, dya, dyb, aa, ab)


def pack(tk, mixer_in, state, query, keyval, step, mixer_out, output):
    width = mixer_in.shape[1]
    cols = 2 * mixer_in.shape[2] + 2 * NS + 256 + PAD
    rows = mixer_out.shape[0] + output.shape[0]
    return pl.pallas_call(
        pack_kernel,
        out_shape=[sds((width, cols), BF16), sds((rows, width), BF16)],
        in_specs=[SM] + [pl.BlockSpec(memory_space=pltpu.HBM)] * 5 + [VM] * 2,
        out_specs=[VM] * 2,
        scratch_shapes=[pltpu.SemaphoreType.DMA((7,))],
        compiler_params=params(8),
        cost_estimate=cost(width * cols, 4 * width * cols),
        name="pack",
    )(tk, mixer_in, state, query, mixer_out, output, keyval, step)


def unpack(packed, inner):
    rows, cols = packed.shape
    heads = cols - 3 * inner - 128
    return pl.pallas_call(
        functools.partial(unpack_kernel, inner),
        out_shape=[
            sds((2, rows, inner), F32),
            sds((rows, 128), F32),
            sds((inner, rows), F32),
            sds((heads, rows), F32),
        ],
        in_specs=[VM],
        out_specs=[VM] * 4,
        compiler_params=params(8),
        cost_estimate=cost(rows * cols, 6 * rows * cols),
        name="unpack",
    )(packed)


def gather(half):
    return (half, lax.ppermute(half, "tensor", CORE))


def scatter(keep, send):
    recv = lax.ppermute(send, "tensor", CORE)
    pair = (keep.astype(F32) + recv.astype(F32)).astype(BF16)
    return (pair, lax.ppermute(pair, "tensor", FAR))


def in_turn(work, pieces):
    results = []
    for m, piece in enumerate(pieces):
        if results:
            pair = results[-1][0]
            pair, piece = lax.optimization_barrier((pair, piece))
        results.append(work(m, piece))
    return results


def rope_tables(length):
    half = AD // 2
    freq = np.float32(ROPE_BASE) ** (
        -(np.arange(half, dtype=np.float32) * np.float32(2.0) / np.float32(AD))
    )
    angles = np.arange(length, dtype=np.float32)[:, None] * freq[None, :].astype(np.float32)
    cos = np.cos(angles).astype(np.float32)
    sin = np.sin(angles).astype(np.float32)
    cos_h = np.concatenate([cos, cos], axis=1)
    sin_h = np.concatenate([-sin, sin], axis=1)
    return np.concatenate(
        [np.concatenate([cos_h, cos_h], axis=1), np.concatenate([sin_h, sin_h], axis=1)], axis=0
    )


def per_device(
    inputs,
    cotangent,
    segment_ids,
    norm_gains,
    mixer_in,
    state_proj,
    step_proj,
    conv_inner,
    conv_state,
    head_params,
    mixer_out,
    query_proj,
    keyval_proj,
    output_proj,
    gate_up,
    down_proj,
):
    section_now = lax.axis_index("section")
    tensor_now = lax.axis_index("tensor")
    dp_count = lax.axis_size("dp")
    tensor_count = lax.axis_size("tensor")
    micro_count = inputs.shape[0]
    width = inputs.shape[3]
    length = segment_ids.shape[2]
    inner = mixer_in.shape[3]
    heads_here = inner // HD
    units = down_proj.shape[1]
    micros = range(micro_count)

    gains = norm_gains[0].astype(F32)
    query_heads = query_proj.shape[2] // AD
    key_group = tensor_now * query_heads // (AH // KVH)
    core, far_at = tensor_now % 2, tensor_now // 2
    t = jnp.stack([core, key_group]).astype(jnp.int32)
    wcat, wout = pack(
        t,
        mixer_in[0],
        state_proj[0],
        query_proj[0],
        keyval_proj[0],
        step_proj[0],
        mixer_out[0],
        output_proj[0],
    )
    taps = jnp.concatenate([conv_inner[0], conv_state[0, 0], conv_state[0, 1]], axis=-1).astype(F32)
    chans = inner + 2 * NS
    taps = jnp.concatenate(
        [
            jnp.pad(taps, ((0, 0), (0, width - chans))),
            jnp.pad(jnp.repeat(head_params[0, 2], HD), (0, width - inner))[None],
            gains[0:1],
            jnp.zeros((2, width), F32),
        ],
        axis=0,
    )
    heads = jnp.pad(head_params[0].T, ((0, 8 - heads_here), (0, PAD - 3)))
    weights = dict(wcat=wcat, wout=wout, taps=taps, wgu=gate_up[0], wd=down_proj[0])
    gain1, gain2 = gains[0].reshape(1, 1, width), gains[1].reshape(1, 1, width)
    rope = jnp.asarray(rope_tables(length))
    tables = [
        jnp.concatenate(
            [
                rope,
                jnp.broadcast_to(segment_ids[m, 0].astype(F32)[:, None], (length, PAD)),
                heads,
            ],
            axis=0,
        )
        for m in micros
    ]

    def halves(own):
        far = lax.ppermute(own, "tensor", FAR)
        both = jnp.where(
            far_at == 0, jnp.stack([own, far], axis=1), jnp.stack([far, own], axis=1)
        )
        return [both[m] for m in micros]

    def own_of(half):
        return lax.dynamic_index_in_dim(half, far_at, 0, keepdims=False)

    def forward(x_own):
        pieces = [gather(x_own[m]) for m in micros]
        parts = in_turn(lambda m, p: scatter(*mixer_fwd(t, p, weights, tables[m])), pieces)
        resid, n2 = zip(*[resid_norm(x_own[m], parts[m], gain2) for m in micros])
        n_pieces = [gather(n2[m]) for m in micros]
        outs = in_turn(lambda m, p: scatter(*ffn_fwd(t, p, weights)), n_pieces)
        result = [
            (resid[m] + (outs[m][0].astype(F32) + outs[m][1].astype(F32))).astype(BF16)
            for m in micros
        ]
        return result, pieces, n_pieces, resid

    def backward(go, saved, x_own, last_pass):
        pieces, n_pieces, resid = saved
        g_pieces = [gather(go[m]) for m in micros]

        def ffn_part(m, grads):
            made = ffn_bwd(t, n_pieces[m], grads, weights, last_pass)
            sent = made[:2]
            made_all.append(made)
            if last_pass and len(made_all) == micro_count:
                g_ffn = wgrad_ffn([(k[2], k[5], k[3], k[4]) for k in made_all])
                sent, g_ffn = lax.optimization_barrier((sent, g_ffn))
                g_all.append(g_ffn)
            return scatter(*sent)

        made_all, g_all = [], []
        parts = in_turn(ffn_part, g_pieces)
        mid = [norm_bwd(resid[m], parts[m], gain2, go[m]) for m in micros]
        d_pieces = [gather(mid[m][1]) for m in micros]

        def mix_part(m, grads):
            made = mixer_bwd(t, pieces[m], grads, weights, tables[m], inner, last_pass)
            return scatter(*made[:2]) + (made,)

        mix_all = in_turn(mix_part, d_pieces)
        mix = [got[2] for got in mix_all]
        parts1 = [got[:2] for got in mix_all]
        low = [norm_bwd(x_own[m], parts1[m], gain1, mid[m][0]) for m in micros]
        return [low[m][1] for m in micros], g_all, mix, mid, low

    first = halves(inputs[:, 0])
    top = halves(cotangent[:, 0])

    out0, _, _, _ = forward(first)
    received = [lax.ppermute(out0[m], "section", [(0, 1)]) for m in micros]
    x_own = [jnp.where(section_now == 0, first[m], received[m]) for m in micros]
    out1, pieces, n_pieces, resid = forward(x_own)
    saved = (pieces, n_pieces, resid)
    grad1, _, _, _, _ = backward(top, saved, x_own, False)
    grad_in = [lax.ppermute(grad1[m], "section", [(1, 0)]) for m in micros]
    go = [jnp.where(section_now == 1, top[m], grad_in[m]) for m in micros]
    d_low, (g_ffn,), mix, mid, low = backward(go, saved, x_own, True)

    rows16 = width // (dp_count * tensor_count)
    r_ffn = lax.psum_scatter(g_ffn, "dp", scatter_dimension=0, tiled=True)
    g_mix, keep, send, g_step = wgrad_mix(
        t, [(mix[m][2], mix[m][5], mix[m][3], mix[m][4]) for m in micros], inner, rows16
    )
    small = sum(mix[m][6] for m in micros)
    headg = sum(mix[m][7] for m in micros)
    d_skip = small[4, :inner].reshape(heads_here, HD).sum(axis=1)
    over_all = jnp.concatenate(
        [
            sum(low[m][2] for m in micros)[0, 0] * 0.5,
            sum(mid[m][2] for m in micros)[0, 0] * 0.5,
            small[:TAPS, inner:].reshape(-1),
        ]
    )
    per_head = jnp.concatenate(
        [
            small[:TAPS, :inner].reshape(-1),
            headg[:heads_here, 0],
            headg[:heads_here, 1],
            d_skip,
        ]
    )
    split_at = over_all.shape[0]
    vector = jnp.concatenate([over_all, per_head])
    turns = [vector] + [
        lax.ppermute(vector, "dp", [(i, (i + turn) % dp_count) for i in range(dp_count)])
        for turn in range(1, dp_count)
    ]
    while len(turns) > 1:
        half = len(turns) // 2
        turns = [turns[k] + turns[k + half] for k in range(half)]
    vector = turns[0]
    recv = lax.ppermute(send, "tensor", CORE)
    pair = keep.astype(F32) + recv.astype(F32)
    last = lax.ppermute(
        lax.dynamic_index_in_dim(pair, 1 - far_at, 0, keepdims=False).astype(BF16), "tensor", FAR
    )
    shared = own_of(pair) + last.astype(F32)
    g_mix, r_ffn, d_low = lax.optimization_barrier((g_mix, r_ffn, d_low))
    r_mix = lax.psum_scatter(g_mix, "dp", scatter_dimension=0, tiled=True)
    cols = shared.shape[1]
    step_sum = g_step.reshape(8, dp_count, -1).transpose(1, 0, 2).reshape(dp_count, -1, cols)
    shared = jnp.concatenate([shared.reshape(dp_count, rows16, cols), step_sum], axis=1)
    step_to = dp_count // 2
    while step_to:
        shared = shared.reshape(2, -1, *shared.shape[1:])
        side = lax.axis_index("dp") // step_to % 2
        give = lax.dynamic_index_in_dim(shared, 1 - side, 0, keepdims=False).astype(BF16)
        got = lax.ppermute(give, "dp", [(i, i ^ step_to) for i in range(dp_count)])
        shared = lax.dynamic_index_in_dim(shared, side, 0, keepdims=False) + got.astype(F32)
        step_to //= 2
    shared = shared.reshape(-1, cols)
    r_shared = shared[:rows16]
    grad_step = shared[rows16:].reshape(8, -1)[:heads_here].T

    over_all, per_head = vector[:split_at], vector[split_at:]
    over_all = over_all + lax.ppermute(over_all, "tensor", CORE)
    over_all = over_all + lax.ppermute(over_all, "tensor", FAR)
    place = lax.axis_index("dp") * tensor_count + tensor_now
    pick = functools.partial(lax.dynamic_slice_in_dim, axis=1)
    grad_gains = pick(over_all[: 2 * width].reshape(2, width), place * rows16, rows16)
    state_taps = over_all[2 * width :].reshape(TAPS, 2, NS).transpose(1, 0, 2)
    each = NS // (dp_count * tensor_count)
    grad_conv_state = lax.dynamic_slice_in_dim(state_taps, place * each, each, axis=2)
    grad_conv_inner = per_head[: TAPS * inner].reshape(TAPS, inner)
    grad_heads = per_head[TAPS * inner :].reshape(3, heads_here)

    r_ffn = r_ffn.astype(F32)
    grad_gate_up = jnp.stack([r_ffn[:, :units], r_ffn[:, units : 2 * units]])
    grad_down = r_ffn[:, 2 * units :].T
    grad_mixer_in, grad_query, grad_mixer_out, grad_output = unpack(r_mix, inner)
    grad_state = jnp.stack([r_shared[:, :NS], r_shared[:, NS : 2 * NS]])
    grad_keyval = r_shared[:, 2 * NS :]
    return (
        jnp.stack([own_of(h) for h in out1])[None, :, None],
        jnp.stack([own_of(h) for h in d_low])[None, :, None],
        grad_gains[None],
        grad_mixer_in[None],
        grad_state[None],
        grad_step[None],
        grad_conv_inner[None],
        grad_conv_state[None],
        grad_heads[None],
        grad_mixer_out[None],
        grad_query[None],
        grad_keyval[None],
        grad_output[None],
        grad_gate_up[None],
        grad_down[None],
    )


def solution(mesh):
    placed = (
        P(None, "dp", "tensor", None),
        P(None, "dp", "tensor", None),
        P(None, "dp", None),
        P("section", None, None),
        P("section", None, None, "tensor"),
        P("section", None, None, None),
        P("section", None, "tensor"),
        P("section", None, "tensor"),
        P("section", None, None, None),
        P("section", None, "tensor"),
        P("section", "tensor", None),
        P("section", None, "tensor"),
        P("section", None, None),
        P("section", "tensor", None),
        P("section", None, None, "tensor"),
        P("section", "tensor", None),
    )
    return jax.shard_map(
        per_device,
        mesh=mesh,
        in_specs=placed,
        out_specs=(
            P("section", None, "dp", "tensor", None),
            P("section", None, "dp", "tensor", None),
            P("section", None, ("dp", "tensor")),
            P("section", None, "dp", "tensor"),
            P("section", None, ("dp", "tensor"), None),
            P("section", "dp", "tensor"),
            P("section", None, "tensor"),
            P("section", None, None, ("dp", "tensor")),
            P("section", None, "tensor"),
            P("section", "tensor", "dp"),
            P("section", "dp", "tensor"),
            P("section", ("dp", "tensor"), None),
            P("section", "tensor", "dp"),
            P("section", None, "dp", "tensor"),
            P("section", "tensor", "dp"),
        ),
        check_vma=False,
    )
```

```python
import functools

import jax
import jax.numpy as jnp
import numpy as np
from jax import lax
from jax.experimental import pallas as pl
from jax.experimental.pallas import tpu as pltpu
from jax.sharding import PartitionSpec as P

HD = 64
NS = 128
AH = 8
KVH = 2
AD = 64
TAPS = 4
PAD = 128

EPS = 1e-06
ROPE_BASE = 100000000000.0
NEG = -1e30

F32 = jnp.float32
BF16 = jnp.bfloat16
HIGH = lax.Precision.HIGHEST
MIB = 1024 * 1024

CORE = [(i, i ^ 1) for i in range(4)]
FAR = [(i, i ^ 2) for i in range(4)]


def dot_nn(a, b, precision=None):
    return lax.dot_general(
        a, b, (((1,), (0,)), ((), ())), preferred_element_type=F32, precision=precision
    )


def dot_nt(a, b):
    return lax.dot_general(a, b, (((1,), (1,)), ((), ())), preferred_element_type=F32)


def dot_tn(a, b):
    return lax.dot_general(a, b, (((0,), (0,)), ((), ())), preferred_element_type=F32)


def sigmoid(a):
    return 1.0 / (1.0 + jnp.exp(-a))


def silu_slope(a, s):
    return s * (1.0 + a * (1.0 - s))


def assemble(core, dst, half, other):
    dst[core] = half[0]
    dst[2 + core] = half[1]
    dst[1 - core] = other[0]
    dst[3 - core] = other[1]


def rows_of(ref):
    blocks, rows, width = ref.shape
    return ref[...].reshape(blocks * rows, width)


def give_parts(core, full, scr, keep_ref, send_ref):
    scr[...] = full.astype(BF16).reshape(scr.shape)
    keep_ref[0] = scr[core]
    keep_ref[1] = scr[2 + core]
    send_ref[0] = scr[1 - core]
    send_ref[1] = scr[3 - core]


def lane_parity(rows, width=128):
    return lax.broadcasted_iota(jnp.int32, (rows, width), 1)


def partner(a):
    lane = lax.broadcasted_iota(jnp.int32, a.shape, 1)
    return jnp.where((lane & 32) == 0, pltpu.roll(a, 96, 1), pltpu.roll(a, 32, 1))


def shift_down(a, k):
    return a if k == 0 else pltpu.roll(a, k, 0)


def shift_up(a, k):
    return a if k == 0 else pltpu.roll(a, a.shape[0] - k, 0)


def mixer_front(xs, taps, wcat, table):
    length = xs.shape[0]
    inner = (wcat.shape[1] - 2 * NS - 256 - PAD) // 2
    chans = inner + 2 * NS
    cos_q, sin_q = table[0:length], table[length : 2 * length]
    seg = table[2 * length : 3 * length]
    seg_rows = jnp.transpose(seg)
    heads = table[3 * length : 3 * length + 8]
    r = lax.rsqrt(jnp.mean(xs * xs, axis=-1, keepdims=True) + EPS)
    normed = (xs * r * taps[5:6, :]).astype(BF16)
    proj = dot_nn(normed, wcat[...])
    z = proj[:, :inner]
    v = proj[:, inner : 2 * inner + 2 * NS]
    place = lax.broadcasted_iota(jnp.int32, (length, 1), 0)
    keeps = []
    for k in range(TAPS):
        earlier = shift_down(seg, k)
        same = (place >= k) & (earlier[:, 0:1] == seg[:, 0:1])
        keeps.append(jnp.where(same, 1.0, 0.0))
    pre = taps[0:1, :chans] * v
    for k in range(1, TAPS):
        pre = pre + taps[k : k + 1, :chans] * (shift_down(v, k) * keeps[k])
    psig = sigmoid(pre)
    conv = pre * psig
    xc = conv[:, :inner]
    b_low = conv[:, inner : inner + NS].astype(BF16)
    c_low = conv[:, inner + NS :].astype(BF16)
    gram = dot_nt(c_low, b_low)
    base = 2 * inner + 2 * NS
    q_raw = proj[:, base : base + 128]
    kv_raw = proj[:, base + 128 : base + 256]
    step_cols = proj[:, base + 256 :]
    raw = jnp.transpose(step_cols)[:8] + heads[:, 0:1]
    step = jnp.maximum(raw, 0.0) + jnp.log1p(jnp.exp(-jnp.abs(raw)))
    rate = jnp.exp(heads[:, 1:2])
    row = lax.broadcasted_iota(jnp.int32, (length, length), 0)
    col = lax.broadcasted_iota(jnp.int32, (length, length), 1)
    upper = jnp.where(row <= col, 1.0, 0.0)
    level = dot_nn(-rate * step, upper, HIGH)
    level_cols = jnp.transpose(
        jnp.concatenate([level, jnp.zeros((PAD - 8, length), F32)], axis=0)
    )
    allowed = (row >= col) & (seg[:, 0:1] == seg_rows[0:1, :])
    lane = lane_parity(length)
    low_half = lane < 64
    cos_kv = jnp.where(low_half, cos_q, 1.0)
    sin_kv = jnp.where(low_half, sin_q, 0.0)
    q_rot = q_raw * cos_q + partner(q_raw) * sin_q
    kv_rot = kv_raw * cos_kv + partner(kv_raw) * sin_kv
    q01 = q_rot.astype(BF16)
    q10 = pltpu.roll(q_rot, 64, 1).astype(BF16)
    kv = kv_rot.astype(BF16)
    vk = pltpu.roll(kv_rot, 64, 1).astype(BF16)
    zero = jnp.zeros((length, 128), BF16)

    def lo(a):
        return jnp.where(low_half, a, zero)

    def hi(a):
        return jnp.where(low_half, zero, a)

    return dict(
        normed=normed, z=z, v=v, keeps=keeps, pre=pre, psig=psig, xc=xc, b_low=b_low,
        c_low=c_low, gram=gram, raw=raw, step=step, rate=rate, level=level,
        level_cols=level_cols, allowed=allowed, q01=q01, q10=q10, kv=kv, vk=vk, lo=lo,
        hi=hi, inner=inner, length=length, row=row, col=col, rope=(cos_q, sin_q, cos_kv, sin_kv),
    )


def decay_of(f, h):
    diff = f["level_cols"][:, h : h + 1] - f["level"][h : h + 1, :]
    return jnp.exp(jnp.where(f["allowed"], diff, NEG))


def probs_of(f, h):
    lo, hi = f["lo"], f["hi"]
    qh = f["q01"] if h == 0 else f["q10"]
    scores = jnp.where(f["allowed"], dot_nt(lo(qh), f["kv"]) * (AD ** (-0.5)), NEG)
    peak = jnp.max(scores, axis=-1, keepdims=True)
    powers = jnp.exp(scores - peak)
    return powers / jnp.sum(powers, axis=-1, keepdims=True)


def mixer_fwd_kernel(
    t_ref, half, other, taps, wcat, wout, table, keep_ref, send_ref, x_scr, act, out_scr
):
    t = t_ref[0]
    assemble(t, x_scr, half, other)
    f = mixer_front(rows_of(x_scr).astype(F32), taps, wcat, table)
    lo, hi, inner = f["lo"], f["hi"], f["inner"]
    for p in range(inner // 128):
        cs = slice(128 * p, 128 * p + 128)
        xp = f["xc"][:, cs]
        xl = xp.astype(BF16)
        y = taps[4:5, cs] * xp
        for j, side in enumerate((lo, hi)):
            h = 2 * p + j
            w = f["gram"] * decay_of(f, h) * f["step"][h : h + 1, :]
            y = y + dot_nn(w.astype(BF16), side(xl))
        z = f["z"][:, cs]
        act[:, cs] = (y * (z * sigmoid(z))).astype(BF16)
    att = dot_nn(probs_of(f, 0).astype(BF16), lo(f["vk"]))
    att = att + dot_nn(probs_of(f, 1).astype(BF16), hi(f["kv"]))
    act[:, inner : inner + 128] = att.astype(BF16)
    give_parts(t, dot_nn(act[...], wout[...]), out_scr, keep_ref, send_ref)


def mixer_bwd_kernel(
    t_ref, half, other, g_half, g_other, taps, wcat, wout, table,
    keep_ref, send_ref, normed_ref, dy, act, dm_ref, small_ref, headg_ref,
    x_scr, dm_scr, out_scr,
):
    t = t_ref[0]
    assemble(t, x_scr, half, other)
    assemble(t, dm_scr, g_half, g_other)
    f = mixer_front(rows_of(x_scr).astype(F32), taps, wcat, table)
    lo, hi, inner, length = f["lo"], f["hi"], f["inner"], f["length"]
    normed_ref[...] = f["normed"]
    dm = rows_of(dm_scr)
    dm_ref[...] = dm
    dact = dot_nt(dm, wout[...])
    gram, step, rate = f["gram"], f["step"], f["rate"]
    lane = lax.broadcasted_iota(jnp.int32, (length, PAD), 1)
    sub = lax.broadcasted_iota(jnp.int32, (8, length), 0)
    d_gram = jnp.zeros((length, length), F32)
    row_sums = jnp.zeros((length, PAD), F32)
    d_step = jnp.zeros((8, length), F32)
    small_ref[...] = jnp.zeros_like(small_ref)
    d_parts = []
    for p in range(inner // 128):
        cs = slice(128 * p, 128 * p + 128)
        xp = f["xc"][:, cs]
        xl = xp.astype(BF16)
        z = f["z"][:, cs]
        zs = sigmoid(z)
        dg = dact[:, cs]
        ds_low = (dg * (z * zs)).astype(BF16)
        ds = ds_low.astype(F32)
        skip = taps[4:5, cs]
        y = skip * xp
        dxc = skip * ds
        for j, side in enumerate((lo, hi)):
            h = 2 * p + j
            e = decay_of(f, h)
            step_h = step[h : h + 1, :]
            w_low = (gram * e * step_h).astype(BF16)
            ds_h = side(ds_low)
            y = y + dot_nn(w_low, side(xl))
            dxc = dxc + dot_tn(w_low, ds_h)
            te = dot_nt(ds_h, xl) * e
            d_gram = d_gram + te * step_h
            tg = te * gram
            d_step = jnp.where(sub == h, jnp.sum(tg, axis=0, keepdims=True), d_step)
            row_sums = jnp.where(
                lane == h, jnp.sum(tg * step_h, axis=1, keepdims=True), row_sums
            )
        act[:, cs] = (y * (z * zs)).astype(BF16)
        dy[:, cs] = (dg * y * silu_slope(z, zs)).astype(BF16)
        small_ref[4:5, cs] = jnp.sum(ds * xp, axis=0, keepdims=True)
        d_parts.append(dxc)
    d_level = jnp.transpose(row_sums)[:8] - step * d_step
    later = jnp.where(f["row"] >= f["col"], 1.0, 0.0)
    tail = dot_nn(d_level, later, HIGH)
    d_step = d_step - rate * tail
    d_raw = d_step * sigmoid(f["raw"])
    d_decay = -rate * jnp.sum(step * tail, axis=1, keepdims=True)
    d_bias = jnp.sum(d_raw, axis=1, keepdims=True)
    lane8 = lax.broadcasted_iota(jnp.int32, (8, PAD), 1)
    headg_ref[...] = jnp.where(lane8 == 0, d_bias, jnp.where(lane8 == 1, d_decay, 0.0))
    base = 2 * inner + 2 * NS
    dy[:, base + 256 : base + 384] = jnp.transpose(
        jnp.concatenate([d_raw, jnp.zeros((PAD - 8, length), F32)], axis=0)
    ).astype(BF16)
    dg_low = d_gram.astype(BF16)
    d_parts.append(dot_tn(dg_low, f["c_low"]))
    d_parts.append(dot_nn(dg_low, f["b_low"]))
    for p, part in enumerate(d_parts):
        cs = slice(128 * p, 128 * p + 128)
        dp = part * silu_slope(f["pre"][:, cs], f["psig"][:, cs])
        v = f["v"][:, cs]
        dv = taps[0:1, cs] * dp
        small_ref[0:1, cs] = jnp.sum(dp * v, axis=0, keepdims=True)
        for k in range(1, TAPS):
            kept = dp * f["keeps"][k]
            dv = dv + taps[k : k + 1, cs] * shift_up(kept, k)
            small_ref[k : k + 1, cs] = jnp.sum(kept * shift_down(v, k), axis=0, keepdims=True)
        dy[:, inner + 128 * p : inner + 128 * p + 128] = dv.astype(BF16)
    da01f = dact[:, inner : inner + 128]
    da01 = da01f.astype(BF16)
    da10 = pltpu.roll(da01f, 64, 1).astype(BF16)
    p0 = probs_of(f, 0)
    p1 = probs_of(f, 1)
    p0l, p1l = p0.astype(BF16), p1.astype(BF16)
    att = dot_nn(p0l, lo(f["vk"])) + dot_nn(p1l, hi(f["kv"]))
    act[:, inner : inner + 128] = att.astype(BF16)
    d_value = dot_tn(p0l, hi(da10)) + dot_tn(p1l, hi(da01))
    dp0 = dot_nt(lo(da01), f["vk"])
    dp1 = dot_nt(hi(da01), f["kv"])
    ds0 = (p0 * (dp0 - jnp.sum(p0 * dp0, axis=-1, keepdims=True))).astype(BF16)
    ds1 = (p1 * (dp1 - jnp.sum(p1 * dp1, axis=-1, keepdims=True))).astype(BF16)
    scale = AD ** (-0.5)
    dq = (dot_nn(ds0, lo(f["kv"])) + dot_nn(ds1, hi(f["vk"]))) * scale
    dkv = (dot_tn(ds0, lo(f["q01"])) + dot_tn(ds1, lo(f["q10"]))) * scale + d_value
    cos_q, sin_q, cos_kv, sin_kv = f["rope"]
    dy[:, base : base + 128] = (dq * cos_q - partner(dq) * sin_q).astype(BF16)
    dy[:, base + 128 : base + 256] = (dkv * cos_kv - partner(dkv) * sin_kv).astype(BF16)
    give_parts(t, dot_nt(dy[...], wcat[...]), out_scr, keep_ref, send_ref)


def ffn_fwd_kernel(
    t_ref, half, other, wgu, wd, keep_ref, send_ref, n_scr, out_scr
):
    t = t_ref[0]
    assemble(t, n_scr, half, other)
    n2 = rows_of(n_scr)
    g = dot_nn(n2, wgu[0])
    u = dot_nn(n2, wgu[1])
    hidden = (g * sigmoid(g) * u).astype(BF16)
    give_parts(t, dot_nn(hidden, wd[...]), out_scr, keep_ref, send_ref)


def ffn_bwd_kernel(
    t_ref, half, other, g_half, g_other, wgu, wd,
    keep_ref, send_ref, n_ref, dgu, hid_ref, go_ref, n_scr, go_scr, out_scr,
):
    t = t_ref[0]
    assemble(t, n_scr, half, other)
    assemble(t, go_scr, g_half, g_other)
    n2 = rows_of(n_scr)
    go = rows_of(go_scr)
    n_ref[...] = n2
    go_ref[...] = go
    width = wd.shape[0]
    g = dot_nn(n2, wgu[0])
    u = dot_nn(n2, wgu[1])
    dh = dot_nt(go, wd[...])
    s = sigmoid(g)
    act = g * s
    hid_ref[...] = (act * u).astype(BF16)
    dg = (dh * u * silu_slope(g, s)).astype(BF16)
    du = (dh * act).astype(BF16)
    dgu[:, :width] = dg
    dgu[:, width:] = du
    give_parts(t, dot_nt(dg, wgu[0]) + dot_nt(du, wgu[1]), out_scr, keep_ref, send_ref)


def resid_norm_kernel(x, pair, far, gain, resid_ref, n_ref):
    a = x[...].astype(F32) + (pair[...].astype(F32) + far[...].astype(F32))
    resid_ref[...] = a
    r = lax.rsqrt(jnp.mean(a * a, axis=-1, keepdims=True) + EPS)
    n_ref[...] = (a * r * gain[...]).astype(BF16)


def norm_bwd_kernel(a_ref, pair, far, gain, base, d_ref, low_ref, dgain_ref):
    a = a_ref[...].astype(F32)
    dn = pair[...].astype(F32) + far[...].astype(F32)
    r = lax.rsqrt(jnp.mean(a * a, axis=-1, keepdims=True) + EPS)
    dgain_ref[...] = jnp.sum(dn * a * r, axis=(0, 1), keepdims=True)
    dng = dn * gain[...]
    inner = jnp.mean(dng * a, axis=-1, keepdims=True)
    d = base[...].astype(F32) + (r * dng - a * (r * r * r) * inner)
    d_ref[...] = d
    low_ref[...] = d.astype(BF16)


def wgrad_ffn_kernel(na, nb, ga, gb, dgua, dgub, ha, hb, out):
    width = dgua.shape[1]
    out[:, :width] = (dot_tn(na[...], dgua[...]) + dot_tn(nb[...], dgub[...])).astype(BF16)
    out[:, width:] = (dot_tn(ga[...], ha[...]) + dot_tn(gb[...], hb[...])).astype(BF16)


def wgrad_mix_kernel(inner, t_ref, na, nb, ga, gb, dya, dyb, aa, ab, out, keep, send, step, scr):
    t, kv_head = t_ref[0], t_ref[1]
    zu = 2 * inner
    bc = zu + 2 * NS
    full = dot_tn(na[...], dya[...]) + dot_tn(nb[...], dyb[...])
    out[:, :zu] = full[:, :zu].astype(BF16)
    out[:, zu : zu + 128] = full[:, bc : bc + 128].astype(BF16)
    step[...] = jnp.transpose(full[:, bc + 256 :])[:8]
    out[:, zu + 128 :] = (dot_tn(ga[...], aa[...]) + dot_tn(gb[...], ab[...])).astype(BF16)
    kv = full[:, bc + 128 : bc + 256]
    vk = pltpu.roll(kv, 64, 1)
    low_half = lane_parity(kv.shape[0]) < 64
    first = kv_head == 0
    k_pair = jnp.where(low_half == first, jnp.where(first, kv, vk), 0.0)
    v_pair = jnp.where(low_half == first, jnp.where(first, vk, kv), 0.0)
    shared = jnp.concatenate([full[:, zu:bc], k_pair, v_pair], axis=1).astype(BF16)
    groups, blocks, rows, cols = scr.shape
    scr[...] = shared.reshape(groups, blocks, rows, cols)
    for g in range(groups):
        at = slice(g * rows, (g + 1) * rows)
        keep[0, at] = scr[g, t]
        keep[1, at] = scr[g, 2 + t]
        send[0, at] = scr[g, 1 - t]
        send[1, at] = scr[g, 3 - t]


def pack_kernel(
    t_ref, mixer_in, state, query, mixer_out, output, keyval, step, wcat, wout, sems
):
    inner = mixer_in.shape[2]
    at = 2 * inner
    end = at + 2 * NS
    moves = [
        (mixer_in.at[0], wcat.at[:, pl.ds(0, inner)]),
        (mixer_in.at[1], wcat.at[:, pl.ds(inner, inner)]),
        (state.at[0], wcat.at[:, pl.ds(at, NS)]),
        (state.at[1], wcat.at[:, pl.ds(at + NS, NS)]),
        (query, wcat.at[:, pl.ds(end, 128)]),
        (mixer_out, wout.at[pl.ds(0, inner)]),
        (output, wout.at[pl.ds(inner, output.shape[0])]),
    ]
    copies = [pltpu.make_async_copy(a, b, sems.at[i]) for i, (a, b) in enumerate(moves)]
    for copy in copies:
        copy.start()
    keys = keyval[:, :128].astype(F32)
    values = keyval[:, 128:].astype(F32)
    low_half = lane_parity(keys.shape[0]) < 64
    first = t_ref[1] == 0
    keys = jnp.where(first, keys, pltpu.roll(keys, 64, 1))
    values = jnp.where(first, pltpu.roll(values, 64, 1), values)
    wcat[:, end + 128 : end + 256] = jnp.where(low_half, keys, values).astype(BF16)
    wcat[:, end + 256 :] = jnp.zeros((keys.shape[0], PAD), BF16)
    wcat[:, end + 256 : end + 256 + step.shape[1]] = step[...]
    for copy in copies:
        copy.wait()


def unpack_kernel(inner, packed, mixer_in, query, mixer_out, output):
    wide = packed[...].astype(F32)
    mixer_in[0] = wide[:, :inner]
    mixer_in[1] = wide[:, inner : 2 * inner]
    query[...] = wide[:, 2 * inner : 2 * inner + 128]
    outs = jnp.transpose(wide[:, 2 * inner + 128 :])
    mixer_out[...] = outs[:inner]
    output[...] = outs[inner:]


VM = pl.BlockSpec(memory_space=pltpu.VMEM)
SM = pl.BlockSpec(memory_space=pltpu.SMEM)


def sds(shape, dtype):
    return jax.ShapeDtypeStruct(tuple(shape), dtype)


def params(mib):
    return pltpu.CompilerParams(vmem_limit_bytes=mib * MIB)


def cost(flops, nbytes, trans=0):
    return pl.CostEstimate(flops=int(flops), bytes_accessed=int(nbytes), transcendentals=int(trans))


def mixer_fwd(t, pieces, w, table):
    _, rows, width = pieces[0].shape
    wcat, wout = w["wcat"], w["wout"]
    length = 4 * rows
    return pl.pallas_call(
        mixer_fwd_kernel,
        out_shape=[sds((2, rows, width), BF16)] * 2,
        in_specs=[SM] + [VM] * 6,
        out_specs=[VM] * 2,
        scratch_shapes=[
            pltpu.VMEM((4, rows, width), BF16),
            pltpu.VMEM((length, wout.shape[0]), BF16),
            pltpu.VMEM((4, rows, width), BF16),
        ],
        compiler_params=params(12),
        cost_estimate=cost(2 * length * (wcat.size + wout.size) * 2, 2 * (wcat.size + wout.size)),
        name="mixer_fwd",
    )(t, *pieces, w["taps"], wcat, wout, table)


def mixer_bwd(t, pieces, grads, w, table, inner, last_pass):
    _, rows, width = pieces[0].shape
    wcat, wout = w["wcat"], w["wout"]
    length = 4 * rows
    kept = [
        ((length, width), BF16),
        ((length, wcat.shape[1]), BF16),
        ((length, wout.shape[0]), BF16),
        ((length, width), BF16),
        ((8, inner + 2 * NS), F32),
        ((8, PAD), F32),
    ]
    sent = [sds((2, rows, width), BF16)] * 2
    blocks = [pltpu.VMEM((4, rows, width), BF16)] * 3
    return pl.pallas_call(
        mixer_bwd_kernel,
        out_shape=sent + ([sds(*k) for k in kept] if last_pass else []),
        in_specs=[SM] + [VM] * 8,
        out_specs=[VM] * (8 if last_pass else 2),
        scratch_shapes=([] if last_pass else [pltpu.VMEM(*k) for k in kept]) + blocks,
        compiler_params=params(16),
        cost_estimate=cost(2 * length * (wcat.size + wout.size) * 5, 2 * (wcat.size + wout.size)),
        name="mixer_bwd",
    )(t, *pieces, *grads, w["taps"], wcat, wout, table)


def ffn_fwd(t, pieces, w):
    _, rows, width = pieces[0].shape
    wgu, wd = w["wgu"], w["wd"]
    return pl.pallas_call(
        ffn_fwd_kernel,
        out_shape=[sds((2, rows, width), BF16)] * 2,
        in_specs=[SM] + [VM] * 4,
        out_specs=[VM] * 2,
        scratch_shapes=[pltpu.VMEM((4, rows, width), BF16)] * 2,
        compiler_params=params(8),
        cost_estimate=cost(8 * rows * (wgu.size + wd.size), 2 * (wgu.size + wd.size)),
        name="ffn_fwd",
    )(t, *pieces, wgu, wd)


def ffn_bwd(t, pieces, grads, w, last_pass):
    _, rows, width = pieces[0].shape
    wgu, wd = w["wgu"], w["wd"]
    length, units = 4 * rows, wd.shape[0]
    kept = [
        ((length, width), BF16),
        ((length, 2 * units), BF16),
        ((length, units), BF16),
        ((length, width), BF16),
    ]
    sent = [sds((2, rows, width), BF16)] * 2
    blocks = [pltpu.VMEM((4, rows, width), BF16)] * 3
    return pl.pallas_call(
        ffn_bwd_kernel,
        out_shape=sent + ([sds(*k) for k in kept] if last_pass else []),
        in_specs=[SM] + [VM] * 6,
        out_specs=[VM] * (6 if last_pass else 2),
        scratch_shapes=([] if last_pass else [pltpu.VMEM(*k) for k in kept]) + blocks,
        compiler_params=params(10),
        cost_estimate=cost(16 * rows * (wgu.size + wd.size), 2 * (wgu.size + wd.size)),
        name="ffn_bwd",
    )(t, *pieces, *grads, wgu, wd)


def whole_block(shape):
    return pl.BlockSpec(shape, lambda i: (0,) * len(shape))


def resid_norm(x, part, gain):
    return pl.pallas_call(
        resid_norm_kernel,
        out_shape=[sds(x.shape, F32), sds(x.shape, BF16)],
        in_specs=[VM] * 4,
        out_specs=[VM] * 2,
        compiler_params=params(4),
        cost_estimate=cost(10 * x.size, 12 * x.size),
        name="resid_norm",
    )(x, *part, gain)


def norm_bwd(a, part, gain, base):
    return pl.pallas_call(
        norm_bwd_kernel,
        out_shape=[sds(a.shape, F32), sds(a.shape, BF16), sds((1, 1, a.shape[2]), F32)],
        in_specs=[VM] * 5,
        out_specs=[VM] * 3,
        compiler_params=params(4),
        cost_estimate=cost(20 * a.size, 16 * a.size),
        name="norm_bwd",
    )(a, *part, gain, base)


def wgrad_ffn(saved):
    (na, ga, dgua, ha), (nb, gb, dgub, hb) = saved
    length, width = na.shape
    cols = dgua.shape[1] + ha.shape[1]
    block = pl.BlockSpec((length, 256), lambda i: (0, i))
    return pl.pallas_call(
        wgrad_ffn_kernel,
        grid=(width // 256,),
        out_shape=pltpu.HBM((width, cols), BF16),
        in_specs=[block] * 4 + [whole_block(dgua.shape)] * 2 + [whole_block(ha.shape)] * 2,
        out_specs=pl.BlockSpec((256, cols), lambda i: (i, 0)),
        compiler_params=params(8),
        cost_estimate=cost(4 * length * width * cols, 2 * width * cols),
        name="wgrad_ffn",
    )(na, nb, ga, gb, dgua, dgub, ha, hb)


def wgrad_mix(tk, saved, inner, rows16):
    (na, ga, dya, aa), (nb, gb, dyb, ab) = saved
    length, width = na.shape
    cols = 2 * inner + 128 + aa.shape[1]
    scols = 2 * NS + 256
    block = pl.BlockSpec((length, 256), lambda i: (0, i))
    part = pl.BlockSpec((2, 64, scols), lambda i: (0, i, 0))
    return pl.pallas_call(
        functools.partial(wgrad_mix_kernel, inner),
        grid=(width // 256,),
        out_shape=[pltpu.HBM((width, cols), BF16)] + [sds((2, width // 4, scols), BF16)] * 2
        + [sds((8, width), F32)],
        in_specs=[SM]
        + [block] * 4
        + [whole_block(dya.shape)] * 2
        + [whole_block(aa.shape)] * 2,
        out_specs=[pl.BlockSpec((256, cols), lambda i: (i, 0)), part, part]
        + [pl.BlockSpec((8, 256), lambda i: (0, i))],
        scratch_shapes=[pltpu.VMEM((64 // rows16, 4, rows16, scols), BF16)],
        compiler_params=params(14),
        cost_estimate=cost(4 * length * width * (cols + 384), 2 * width * (cols + 384)),
        name="wgrad_mix",
    )(tk, na, nb, ga, gb, dya, dyb, aa, ab)


def pack(tk, mixer_in, state, query, keyval, step, mixer_out, output):
    width = mixer_in.shape[1]
    cols = 2 * mixer_in.shape[2] + 2 * NS + 256 + PAD
    rows = mixer_out.shape[0] + output.shape[0]
    return pl.pallas_call(
        pack_kernel,
        out_shape=[sds((width, cols), BF16), sds((rows, width), BF16)],
        in_specs=[SM] + [pl.BlockSpec(memory_space=pltpu.HBM)] * 5 + [VM] * 2,
        out_specs=[VM] * 2,
        scratch_shapes=[pltpu.SemaphoreType.DMA((7,))],
        compiler_params=params(8),
        cost_estimate=cost(width * cols, 4 * width * cols),
        name="pack",
    )(tk, mixer_in, state, query, mixer_out, output, keyval, step)


def unpack(packed, inner):
    rows, cols = packed.shape
    heads = cols - 3 * inner - 128
    return pl.pallas_call(
        functools.partial(unpack_kernel, inner),
        out_shape=[
            sds((2, rows, inner), F32),
            sds((rows, 128), F32),
            sds((inner, rows), F32),
            sds((heads, rows), F32),
        ],
        in_specs=[VM],
        out_specs=[VM] * 4,
        compiler_params=params(8),
        cost_estimate=cost(rows * cols, 6 * rows * cols),
        name="unpack",
    )(packed)


def gather(half):
    return (half, lax.ppermute(half, "tensor", CORE))


def scatter(keep, send):
    recv = lax.ppermute(send, "tensor", CORE)
    pair = (keep.astype(F32) + recv.astype(F32)).astype(BF16)
    return (pair, lax.ppermute(pair, "tensor", FAR))


def in_turn(work, pieces):
    results = []
    for m, piece in enumerate(pieces):
        if results:
            pair = results[-1][0]
            pair, piece = lax.optimization_barrier((pair, piece))
        results.append(work(m, piece))
    return results


def rope_tables(length):
    half = AD // 2
    freq = np.float32(ROPE_BASE) ** (
        -(np.arange(half, dtype=np.float32) * np.float32(2.0) / np.float32(AD))
    )
    angles = np.arange(length, dtype=np.float32)[:, None] * freq[None, :].astype(np.float32)
    cos = np.cos(angles).astype(np.float32)
    sin = np.sin(angles).astype(np.float32)
    cos_h = np.concatenate([cos, cos], axis=1)
    sin_h = np.concatenate([-sin, sin], axis=1)
    return np.concatenate(
        [np.concatenate([cos_h, cos_h], axis=1), np.concatenate([sin_h, sin_h], axis=1)], axis=0
    )


def per_device(
    inputs,
    cotangent,
    segment_ids,
    norm_gains,
    mixer_in,
    state_proj,
    step_proj,
    conv_inner,
    conv_state,
    head_params,
    mixer_out,
    query_proj,
    keyval_proj,
    output_proj,
    gate_up,
    down_proj,
):
    section_now = lax.axis_index("section")
    tensor_now = lax.axis_index("tensor")
    dp_count = lax.axis_size("dp")
    tensor_count = lax.axis_size("tensor")
    micro_count = inputs.shape[0]
    width = inputs.shape[3]
    length = segment_ids.shape[2]
    inner = mixer_in.shape[3]
    heads_here = inner // HD
    units = down_proj.shape[1]
    micros = range(micro_count)

    gains = norm_gains[0].astype(F32)
    query_heads = query_proj.shape[2] // AD
    key_group = tensor_now * query_heads // (AH // KVH)
    core, far_at = tensor_now % 2, tensor_now // 2
    t = jnp.stack([core, key_group]).astype(jnp.int32)
    wcat, wout = pack(
        t,
        mixer_in[0],
        state_proj[0],
        query_proj[0],
        keyval_proj[0],
        step_proj[0],
        mixer_out[0],
        output_proj[0],
    )
    taps = jnp.concatenate([conv_inner[0], conv_state[0, 0], conv_state[0, 1]], axis=-1).astype(F32)
    chans = inner + 2 * NS
    taps = jnp.concatenate(
        [
            jnp.pad(taps, ((0, 0), (0, width - chans))),
            jnp.pad(jnp.repeat(head_params[0, 2], HD), (0, width - inner))[None],
            gains[0:1],
            jnp.zeros((2, width), F32),
        ],
        axis=0,
    )
    heads = jnp.pad(head_params[0].T, ((0, 8 - heads_here), (0, PAD - 3)))
    weights = dict(wcat=wcat, wout=wout, taps=taps, wgu=gate_up[0], wd=down_proj[0])
    gain1, gain2 = gains[0].reshape(1, 1, width), gains[1].reshape(1, 1, width)
    rope = jnp.asarray(rope_tables(length))
    tables = [
        jnp.concatenate(
            [
                rope,
                jnp.broadcast_to(segment_ids[m, 0].astype(F32)[:, None], (length, PAD)),
                heads,
            ],
            axis=0,
        )
        for m in micros
    ]

    def halves(own):
        far = lax.ppermute(own, "tensor", FAR)
        both = jnp.where(
            far_at == 0, jnp.stack([own, far], axis=1), jnp.stack([far, own], axis=1)
        )
        return [both[m] for m in micros]

    def own_of(half):
        return lax.dynamic_index_in_dim(half, far_at, 0, keepdims=False)

    def hop(here, values, pairs, keeps):
        moved = [lax.ppermute(value, "section", pairs) for value in values]
        own, pieces = [], []
        for m in micros:
            value = moved[m]
            if pieces:
                half, other = pieces[-1]
                other, value = lax.optimization_barrier((other, value))
                pieces[-1] = (half, other)
            own.append(jnp.where(section_now == keeps, here[m], value))
            pieces.append(gather(own[m]))
        return own, pieces

    def forward(x_own, pieces):
        parts = in_turn(lambda m, p: scatter(*mixer_fwd(t, p, weights, tables[m])), pieces)
        resid, n2 = zip(*[resid_norm(x_own[m], parts[m], gain2) for m in micros])
        n_pieces = [gather(n2[m]) for m in micros]
        outs = in_turn(lambda m, p: scatter(*ffn_fwd(t, p, weights)), n_pieces)
        result = [
            (resid[m] + (outs[m][0].astype(F32) + outs[m][1].astype(F32))).astype(BF16)
            for m in micros
        ]
        return result, pieces, n_pieces, resid

    def backward(go, g_pieces, saved, x_own, last_pass):
        pieces, n_pieces, resid = saved

        def ffn_part(m, grads):
            made = ffn_bwd(t, n_pieces[m], grads, weights, last_pass)
            sent = made[:2]
            made_all.append(made)
            if last_pass and len(made_all) == micro_count:
                g_ffn = wgrad_ffn([(k[2], k[5], k[3], k[4]) for k in made_all])
                sent, g_ffn = lax.optimization_barrier((sent, g_ffn))
                g_all.append(g_ffn)
            return scatter(*sent)

        made_all, g_all = [], []
        parts = in_turn(ffn_part, g_pieces)
        mid = [norm_bwd(resid[m], parts[m], gain2, go[m]) for m in micros]
        d_pieces = [gather(mid[m][1]) for m in micros]

        def mix_part(m, grads):
            made = mixer_bwd(t, pieces[m], grads, weights, tables[m], inner, last_pass)
            return scatter(*made[:2]) + (made,)

        mix_all = in_turn(mix_part, d_pieces)
        mix = [got[2] for got in mix_all]
        parts1 = [got[:2] for got in mix_all]
        low = [norm_bwd(x_own[m], parts1[m], gain1, mid[m][0]) for m in micros]
        return [low[m][1] for m in micros], g_all, mix, mid, low

    first = halves(inputs[:, 0])
    top = halves(cotangent[:, 0])

    out0, _, _, _ = forward(first, [gather(x) for x in first])
    x_own, x_pieces = hop(first, out0, [(0, 1)], 0)
    out1, pieces, n_pieces, resid = forward(x_own, x_pieces)
    saved = (pieces, n_pieces, resid)
    grad1, _, _, _, _ = backward(top, [gather(g) for g in top], saved, x_own, False)
    go, g_pieces = hop(top, grad1, [(1, 0)], 1)
    d_low, (g_ffn,), mix, mid, low = backward(go, g_pieces, saved, x_own, True)

    rows16 = width // (dp_count * tensor_count)
    r_ffn = lax.psum_scatter(g_ffn, "dp", scatter_dimension=0, tiled=True)
    g_mix, keep, send, g_step = wgrad_mix(
        t, [(mix[m][2], mix[m][5], mix[m][3], mix[m][4]) for m in micros], inner, rows16
    )
    small = sum(mix[m][6] for m in micros)
    headg = sum(mix[m][7] for m in micros)
    d_skip = small[4, :inner].reshape(heads_here, HD).sum(axis=1)
    over_all = jnp.concatenate(
        [
            sum(low[m][2] for m in micros)[0, 0] * 0.5,
            sum(mid[m][2] for m in micros)[0, 0] * 0.5,
            small[:TAPS, inner:].reshape(-1),
        ]
    )
    per_head = jnp.concatenate(
        [
            small[:TAPS, :inner].reshape(-1),
            headg[:heads_here, 0],
            headg[:heads_here, 1],
            d_skip,
        ]
    )
    split_at = over_all.shape[0]
    vector = jnp.concatenate([over_all, per_head])
    turns = [vector] + [
        lax.ppermute(vector, "dp", [(i, (i + turn) % dp_count) for i in range(dp_count)])
        for turn in range(1, dp_count)
    ]
    while len(turns) > 1:
        half = len(turns) // 2
        turns = [turns[k] + turns[k + half] for k in range(half)]
    vector = turns[0]
    recv = lax.ppermute(send, "tensor", CORE)
    pair = keep.astype(F32) + recv.astype(F32)
    last = lax.ppermute(
        lax.dynamic_index_in_dim(pair, 1 - far_at, 0, keepdims=False).astype(BF16), "tensor", FAR
    )
    shared = own_of(pair) + last.astype(F32)
    g_mix, r_ffn, d_low = lax.optimization_barrier((g_mix, r_ffn, d_low))
    r_mix = lax.psum_scatter(g_mix, "dp", scatter_dimension=0, tiled=True)
    cols = shared.shape[1]
    step_sum = g_step.reshape(8, dp_count, -1).transpose(1, 0, 2).reshape(dp_count, -1, cols)
    shared = jnp.concatenate([shared.reshape(dp_count, rows16, cols), step_sum], axis=1)
    step_to = dp_count // 2
    while step_to:
        shared = shared.reshape(2, -1, *shared.shape[1:])
        side = lax.axis_index("dp") // step_to % 2
        give = lax.dynamic_index_in_dim(shared, 1 - side, 0, keepdims=False).astype(BF16)
        got = lax.ppermute(give, "dp", [(i, i ^ step_to) for i in range(dp_count)])
        shared = lax.dynamic_index_in_dim(shared, side, 0, keepdims=False) + got.astype(F32)
        step_to //= 2
    shared = shared.reshape(-1, cols)
    r_shared = shared[:rows16]
    grad_step = shared[rows16:].reshape(8, -1)[:heads_here].T

    over_all, per_head = vector[:split_at], vector[split_at:]
    over_all = over_all + lax.ppermute(over_all, "tensor", CORE)
    over_all = over_all + lax.ppermute(over_all, "tensor", FAR)
    place = lax.axis_index("dp") * tensor_count + tensor_now
    pick = functools.partial(lax.dynamic_slice_in_dim, axis=1)
    grad_gains = pick(over_all[: 2 * width].reshape(2, width), place * rows16, rows16)
    state_taps = over_all[2 * width :].reshape(TAPS, 2, NS).transpose(1, 0, 2)
    each = NS // (dp_count * tensor_count)
    grad_conv_state = lax.dynamic_slice_in_dim(state_taps, place * each, each, axis=2)
    grad_conv_inner = per_head[: TAPS * inner].reshape(TAPS, inner)
    grad_heads = per_head[TAPS * inner :].reshape(3, heads_here)

    r_ffn = r_ffn.astype(F32)
    grad_gate_up = jnp.stack([r_ffn[:, :units], r_ffn[:, units : 2 * units]])
    grad_down = r_ffn[:, 2 * units :].T
    grad_mixer_in, grad_query, grad_mixer_out, grad_output = unpack(r_mix, inner)
    grad_state = jnp.stack([r_shared[:, :NS], r_shared[:, NS : 2 * NS]])
    grad_keyval = r_shared[:, 2 * NS :]
    return (
        jnp.stack([own_of(h) for h in out1])[None, :, None],
        jnp.stack([own_of(h) for h in d_low])[None, :, None],
        grad_gains[None],
        grad_mixer_in[None],
        grad_state[None],
        grad_step[None],
        grad_conv_inner[None],
        grad_conv_state[None],
        grad_heads[None],
        grad_mixer_out[None],
        grad_query[None],
        grad_keyval[None],
        grad_output[None],
        grad_gate_up[None],
        grad_down[None],
    )


def solution(mesh):
    placed = (
        P(None, "dp", "tensor", None),
        P(None, "dp", "tensor", None),
        P(None, "dp", None),
        P("section", None, None),
        P("section", None, None, "tensor"),
        P("section", None, None, None),
        P("section", None, "tensor"),
        P("section", None, "tensor"),
        P("section", None, None, None),
        P("section", None, "tensor"),
        P("section", "tensor", None),
        P("section", None, "tensor"),
        P("section", None, None),
        P("section", "tensor", None),
        P("section", None, None, "tensor"),
        P("section", "tensor", None),
    )
    return jax.shard_map(
        per_device,
        mesh=mesh,
        in_specs=placed,
        out_specs=(
            P("section", None, "dp", "tensor", None),
            P("section", None, "dp", "tensor", None),
            P("section", None, ("dp", "tensor")),
            P("section", None, "dp", "tensor"),
            P("section", None, ("dp", "tensor"), None),
            P("section", "dp", "tensor"),
            P("section", None, "tensor"),
            P("section", None, None, ("dp", "tensor")),
            P("section", None, "tensor"),
            P("section", "tensor", "dp"),
            P("section", "dp", "tensor"),
            P("section", ("dp", "tensor"), None),
            P("section", "tensor", "dp"),
            P("section", None, "dp", "tensor"),
            P("section", "tensor", "dp"),
        ),
        check_vma=False,
    )
```
